128 devices in a mesh: row: 8 (over z, x_lo), col: 16 (over y, x_hi, core).
Axes of the slice: x: 4 (x_hi: 2, x_lo: 2; x = x_hi * 2 + x_lo), y: 4, z: 4, core: 2. Of those that a mesh axis runs over, the one named last changes fastest.
Arguments:
- layer_input: bfloat16 [2048, 6144], P('row', 'col'), may hold values from -6 to 6
- out_grad: bfloat16 [2048, 6144], P('row', 'col'), may hold values from -3 to 3
- pre_act: bfloat16 [2048, 24576], P('col', 'row'), may hold values from -8 to 8
- w_in: bfloat16 [6144, 24576], P('col', 'row'), may hold values from -0.078125 to 0.078125
- w_out: bfloat16 [24576, 6144], P('row', 'col'), may hold values from -0.0390625 to 0.0390625
Outputs:
- input_grad: bfloat16 [2048, 6144], P('row', 'col')
- w_in_grad: bfloat16 [6144, 24576], P('col', 'row')
- w_out_grad: bfloat16 [24576, 6144], P('row', 'col')
- bias_in_grad: float32 [24576], P('row')
- bias_out_grad: float32 [6144], P('col')
The draws below stay inside these ranges and needn't reach their ends.
All inputs are finite; a program needn't handle non-finite values.
Results may differ from the reference program's by a relative error of at most 0.035.
Values may be sent and summed in bfloat16 or wider, within the bound.
No kernel may reach another device: no remote copies, remote signals or barrier semaphores. Data moves between devices by JAX's collectives and lax.ppermute only.
A program may use at most 128 MiB of HBM per device.

```python
import jax
import jax.numpy as jnp
from jax import lax

D = 6144
F = 24576
TOKENS = 2048
N_ROW = 8
N_COL = 16


def block_scale(rng, extent, shards, least, top_value):
    gain, own = 1.0, jax.random.fold_in(rng, 6)
    for position, parts in shards:
        draws = jnp.exp(jax.random.uniform(jax.random.fold_in(own, position), (parts,), jnp.float32, least / len(shards), top_value / len(shards)))
        gain = gain * jnp.repeat(draws, extent[position] // parts).reshape([-1 if axis == position else 1 for axis in range(len(extent))])
    return gain


def centred(key, shape, deviation, limit, pieces=(), kind=jnp.bfloat16):
    result = jax.random.normal(key, shape, jnp.float32) * deviation
    if len(pieces) > 0:
        result = block_scale(key, shape, pieces, -0.22, 0.18) * result
    return jnp.clip(result, min=-limit, max=limit).astype(kind)


def setup_inputs(seed: int = 0) -> dict:
    streams_of = jax.random.split(jax.random.key(seed), 6)
    layer_input = centred(streams_of[0], (TOKENS, D), 1.0, 6.0, ((0, 8), (1, 16)))
    out_grad = centred(streams_of[1], (TOKENS, D), 0.5, 3.0, ((0, 8), (1, 16)))
    pre_act = centred(streams_of[2], (TOKENS, F), 1.5, 8.0, ((0, 16), (1, 8)))
    w_in = centred(streams_of[3], (D, F), D ** -0.5, 0.078125, ((0, 16), (1, 8)))
    w_out = centred(streams_of[4], (F, D), F ** -0.5, 0.0390625, ((0, 8), (1, 16)))
    return {"layer_input": layer_input, "out_grad": out_grad, "pre_act": pre_act, "w_in": w_in, "w_out": w_out}


def gelu_parts(values):
    normal_cdf = 0.5 * (1.0 + lax.erf(values * 0.7071067811865476))
    normal_pdf = jnp.exp(-0.5 * values * values) * 0.3989422804014327
    return values * normal_cdf, normal_cdf + values * normal_pdf


def rounded(values):
    return lax.optimization_barrier(values.astype(jnp.bfloat16)).astype(jnp.float32)


def reference(layer_input, out_grad, pre_act, w_in, w_out):
    activ, slopes = gelu_parts(pre_act.astype(jnp.float32))
    act = activ.astype(jnp.bfloat16)
    width_col = D // N_COL
    act_grad = jnp.zeros((TOKENS, F), jnp.float32)
    for block in range(N_COL):
        lower = block * width_col
        term = lax.dot_general(out_grad[:, lower:lower + width_col], w_out[:, lower:lower + width_col],
                               (((1,), (1,)), ((), ())), preferred_element_type=jnp.float32)
        act_grad = act_grad + rounded(term)
    hidden_grad = (act_grad * slopes).astype(jnp.bfloat16)
    width_row = F // N_ROW
    input_total = jnp.zeros((TOKENS, D), jnp.float32)
    for block in range(N_ROW):
        lower = block * width_row
        term = lax.dot_general(hidden_grad[:, lower:lower + width_row], w_in[:, lower:lower + width_row],
                               (((1,), (1,)), ((), ())), preferred_element_type=jnp.float32)
        input_total = input_total + rounded(term)
    input_grad = input_total.astype(jnp.bfloat16)
    w_in_grad = lax.dot_general(layer_input, hidden_grad, (((0,), (0,)), ((), ())),
                                preferred_element_type=jnp.float32).astype(jnp.bfloat16)
    w_out_grad = lax.dot_general(act, out_grad, (((0,), (0,)), ((), ())),
                                 preferred_element_type=jnp.float32).astype(jnp.bfloat16)
    bias_in_grad = jnp.sum(hidden_grad.astype(jnp.float32), axis=0)
    bias_out_grad = jnp.sum(out_grad.astype(jnp.float32), axis=0)
    return (input_grad, w_in_grad, w_out_grad, bias_in_grad, bias_out_grad)
```

```python
import jax
import jax.numpy as jnp
from jax import lax
from jax.sharding import Mesh, PartitionSpec as P

SIZES = {"z": 4, "xl": 2, "y": 4, "xh": 2, "c": 2}
BF, F32 = jnp.bfloat16, jnp.float32


def gelu_act(v):
    return v * (0.5 * (1.0 + lax.erf(v * 0.7071067811865476)))


def gelu_slope(v):
    normal_cdf = 0.5 * (1.0 + lax.erf(v * 0.7071067811865476))
    normal_pdf = jnp.exp(-0.5 * v * v) * 0.3989422804014327
    return normal_cdf + v * normal_pdf


def shift(x, axis, by):
    n = SIZES[axis]
    return lax.ppermute(x, axis, [(i, (i + by) % n) for i in range(n)])


def flip(x, *axes):
    n = 2 ** len(axes)
    return lax.ppermute(x, axes if len(axes) > 1 else axes[0], [(i, n - 1 - i) for i in range(n)])


def dot_nt(a, b):
    return lax.dot_general(a, b, (((1,), (1,)), ((), ())), preferred_element_type=F32)


def dot_tn(a, b):
    return lax.dot_general(a, b, (((0,), (0,)), ((), ())), preferred_element_type=F32)


def blk(x, i, size, axis):
    return lax.dynamic_slice_in_dim(x, i * size, size, axis)


def put(buf, x, i, axis):
    return lax.dynamic_update_slice_in_dim(buf, x, i * x.shape[axis], axis)


def spread(x, axis, xh, c):
    n = x.shape[axis] // 4
    piece = lambda a, b: blk(x, a * 2 + b, n, axis)
    rec = flip(jnp.stack([piece(xh, 1 - c), piece(1 - xh, 1 - c)]), "c")
    got = flip(jnp.stack([piece(1 - xh, c), rec[1]]), "xh")
    return piece(xh, c), rec[0], got[0], got[1]


def unspread(e0, e1, e2, e3, axis, q):
    got = flip(jnp.stack([e2, e3]), "xh")
    rec = flip(jnp.stack([e1, got[1]]), "c")
    shape = list(e0.shape)
    shape[axis] *= 4
    out = jnp.zeros(shape, e0.dtype)
    for d, part in enumerate((e0, rec[0], got[0], rec[1])):
        out = put(out, part, q ^ d, axis)
    return out


def ring_gather(x, axis, me):
    h = x.shape[0] // 2
    up, down = shift(x, axis, 1), shift(x, axis, -1)
    far = jnp.concatenate([shift(up[:h], axis, 1), shift(down[h:], axis, -1)], 0)
    out = jnp.zeros((4 * x.shape[0], x.shape[1]), x.dtype)
    for k, part in ((0, x), (3, up), (1, down), (2, far)):
        out = put(out, part, (me + k) % 4, 0)
    return out


def ring_scatter(p, axis, me):
    n = p.shape[0] // 4
    h = n // 2
    b = [blk(p, (me + k) % 4, n, 0) for k in range(4)]
    r1 = shift(jnp.concatenate([b[2][:h], b[1][h:]], 0), axis, 1)
    l1 = shift(jnp.concatenate([b[3][:h], b[2][h:]], 0), axis, -1)
    r2 = shift((b[1][:h].astype(F32) + r1[:h].astype(F32)).astype(BF), axis, 1)
    l2 = shift((b[3][h:].astype(F32) + l1[h:].astype(F32)).astype(BF), axis, -1)
    top = b[0][:h].astype(F32) + l1[:h].astype(F32) + r2.astype(F32)
    low = b[0][h:].astype(F32) + r1[h:].astype(F32) + l2.astype(F32)
    return jnp.concatenate([top, low], 0)


def x_gather(g, xl):
    gl, gh, gb = flip(g, "xl"), flip(g, "xh"), flip(g, "xl", "xh")
    first = xl == 0
    top = jnp.concatenate([jnp.where(first, g, gl), jnp.where(first, gh, gb)], 1)
    low = jnp.concatenate([jnp.where(first, gl, g), jnp.where(first, gb, gh)], 1)
    return jnp.concatenate([top, low], 0)


def local(layer_input, out_grad, pre_act, w_in, w_out):
    z, xl, y, xh, c = (lax.axis_index(a) for a in ("z", "xl", "y", "xh", "c"))
    q = xh * 2 + c
    d_own = layer_input.shape[1]

    og = ring_gather(x_gather(out_grad, xl), "z", z)
    og_o = flip(og, "c")
    wo = spread(w_out, 0, xh, c)
    part = dot_nt(og, jnp.concatenate([wo[0], wo[2]], 1)) + dot_nt(og_o, jnp.concatenate([wo[1], wo[3]], 1))
    act_grad = ring_scatter(part.astype(BF), "y", y)

    pieces = spread(pre_act, 1, xh, c)
    pre_own = jnp.zeros((4 * pre_act.shape[0], pieces[0].shape[1]), BF)
    for d, piece in enumerate(pieces):
        pre_own = put(pre_own, piece, q ^ d, 0)
    pre = ring_gather(pre_own, "y", y)

    hidden_own = (act_grad * gelu_slope(pre_own.astype(F32))).astype(BF)
    hidden = ring_gather(hidden_own, "y", y)

    act = gelu_act(pre.astype(F32)).astype(BF)
    go, goo = dot_tn(act, og).astype(BF), dot_tn(act, og_o).astype(BF)
    w_out_grad = unspread(go[:, :d_own], goo[:, :d_own], go[:, d_own:], goo[:, d_own:], 0, q)

    wi = spread(w_in, 1, xh, c)
    ig_o = dot_nt(hidden, jnp.concatenate([wi[1], wi[3]], 0)).astype(BF)
    ig = dot_nt(hidden, jnp.concatenate([wi[0], wi[2]], 0)) + flip(ig_o, "c").astype(F32)
    ig = ring_scatter(ig.astype(BF), "z", z).astype(BF)
    t_own = layer_input.shape[0]
    near, other = blk(ig, xl, t_own, 0), blk(ig, 1 - xl, t_own, 0)
    input_grad = (
        near[:, :d_own].astype(F32)
        + flip(other[:, :d_own], "xl").astype(F32)
        + flip(near[:, d_own:], "xh").astype(F32)
        + flip(other[:, d_own:], "xl", "xh").astype(F32)
    ).astype(BF)

    li = ring_gather(x_gather(layer_input, xl), "z", z)
    li_o = flip(li, "c")
    gi, gio = dot_tn(li, hidden).astype(BF), dot_tn(li_o, hidden).astype(BF)
    w_in_grad = unspread(gi[:d_own], gio[:d_own], gi[d_own:], gio[d_own:], 1, q)

    b0 = jnp.sum(hidden.astype(F32), axis=0)
    b1 = flip(b0, "c")
    b23 = flip(jnp.stack([b0, b1]), "xh")
    bias_in = jnp.zeros((4 * b0.shape[0],), F32)
    for d, part in enumerate((b0, b1, b23[0], b23[1])):
        bias_in = put(bias_in, part, q ^ d, 0)
    bias_out = jnp.sum(og[:, :d_own].astype(F32), axis=0)
    return input_grad, w_in_grad, w_out_grad, bias_in, bias_out


def solution(mesh):
    fine = Mesh(mesh.devices.reshape(tuple(SIZES.values())), tuple(SIZES))
    row, col = ("z", "xl"), ("y", "xh", "c")
    in_specs = (P(row, col), P(row, col), P(col, row), P(col, row), P(row, col))
    out_specs = (P(row, col), P(col, row), P(row, col), P(row), P(col))
    return jax.shard_map(local, mesh=fine, in_specs=in_specs, out_specs=out_specs, check_vma=False)
```

```python
import jax
import jax.numpy as jnp
from jax import lax
from jax.sharding import Mesh, PartitionSpec as P

SIZES = {"z": 4, "xl": 2, "y": 4, "xh": 2, "c": 2}
BF, F32 = jnp.bfloat16, jnp.float32


def gelu_act(v):
    return v * (0.5 * (1.0 + lax.erf(v * 0.7071067811865476)))


def gelu_slope(v):
    normal_cdf = 0.5 * (1.0 + lax.erf(v * 0.7071067811865476))
    normal_pdf = jnp.exp(-0.5 * v * v) * 0.3989422804014327
    return normal_cdf + v * normal_pdf


def shift(x, axis, by):
    n = SIZES[axis]
    return lax.ppermute(x, axis, [(i, (i + by) % n) for i in range(n)])


def flip(x, *axes):
    n = 2 ** len(axes)
    return lax.ppermute(x, axes if len(axes) > 1 else axes[0], [(i, n - 1 - i) for i in range(n)])


def dot_nt(a, b):
    return lax.dot_general(a, b, (((1,), (1,)), ((), ())), preferred_element_type=F32)


def dot_tn(a, b):
    return lax.dot_general(a, b, (((0,), (0,)), ((), ())), preferred_element_type=F32)


def blk(x, i, size, axis):
    return lax.dynamic_slice_in_dim(x, i * size, size, axis)


def put(buf, x, i, axis):
    return lax.dynamic_update_slice_in_dim(buf, x, i * x.shape[axis], axis)


def after(x, *tokens):
    return lax.optimization_barrier((x, *tokens))[0]


def unspread(e0, e1, far, axis):
    n = e0.shape[axis]
    got = flip(far, "xh")
    mine, pass_on = lax.slice_in_dim(got, 0, n, axis=axis), lax.slice_in_dim(got, n, 2 * n, axis=axis)
    rec = flip(jnp.concatenate([e1, pass_on], axis), "c")
    return e0, lax.slice_in_dim(rec, 0, n, axis=axis), mine, lax.slice_in_dim(rec, n, 2 * n, axis=axis)


def lay(parts, axis, q, offset=0, out=None):
    n = parts[0].shape[axis]
    if out is None:
        shape = list(parts[0].shape)
        shape[axis] *= 4
        out, stride = jnp.zeros(shape, parts[0].dtype), n
    else:
        stride = out.shape[axis] // 4
    for d, part in enumerate(parts):
        out = lax.dynamic_update_slice_in_dim(out, part, (q ^ d) * stride + offset, axis)
    return out


def ring_gather(x, axis, me):
    h = x.shape[0] // 2
    up, down = shift(x, axis, 1), shift(x, axis, -1)
    far = jnp.concatenate([shift(up[:h], axis, 1), shift(down[h:], axis, -1)], 0)
    out = jnp.zeros((4 * x.shape[0], x.shape[1]), x.dtype)
    for k, part in ((0, x), (3, up), (1, down), (2, far)):
        out = put(out, part, (me + k) % 4, 0)
    return out


def ring_scatter(p, axis, me):
    n = p.shape[0] // 4
    h = n // 2
    b = [blk(p, (me + k) % 4, n, 0) for k in range(4)]
    r1 = shift(jnp.concatenate([b[2][:h], b[1][h:]], 0), axis, 1)
    l1 = shift(jnp.concatenate([b[3][:h], b[2][h:]], 0), axis, -1)
    r2 = shift((b[1][:h].astype(F32) + r1[:h].astype(F32)).astype(BF), axis, 1)
    l2 = shift((b[3][h:].astype(F32) + l1[h:].astype(F32)).astype(BF), axis, -1)
    top = b[0][:h].astype(F32) + l1[:h].astype(F32) + r2.astype(F32)
    low = b[0][h:].astype(F32) + r1[h:].astype(F32) + l2.astype(F32)
    return jnp.concatenate([top, low], 0)


def x_parts(g):
    return flip(g, "xl"), flip(g, "xh"), flip(g, "xl", "xh")


def x_join(g, parts, xl):
    gl, gh, gb = parts
    first = xl == 0
    top = jnp.concatenate([jnp.where(first, g, gl), jnp.where(first, gh, gb)], 1)
    low = jnp.concatenate([jnp.where(first, gl, g), jnp.where(first, gb, gh)], 1)
    return jnp.concatenate([top, low], 0)


CUTS = (512, 256)


def local(layer_input, out_grad, pre_act, w_in, w_out):
    z, xl, y, xh, c = (lax.axis_index(a) for a in ("z", "xl", "y", "xh", "c"))
    q = xh * 2 + c
    t_own, d_own = layer_input.shape
    f_dev = w_out.shape[0] // 4
    spans = [(0, CUTS[0]), (CUTS[0], f_dev)]

    og_x = x_parts(out_grad)
    og_blk = x_join(out_grad, og_x, xl)

    wo4 = w_out.reshape(2, 2, f_dev, d_own)
    wo_here = lax.dynamic_index_in_dim(wo4, xh, 0, keepdims=False)
    wo_there = lax.dynamic_index_in_dim(wo4, 1 - xh, 0, keepdims=False)
    pick = lambda x, i: lax.dynamic_index_in_dim(x, i, 0, keepdims=False)
    wo0, wo1 = pick(wo_here, c), flip(pick(wo_here, 1 - c), "c")

    pa_here, pa_there = blk(pre_act, xh, 2 * f_dev, 1), blk(pre_act, 1 - xh, 2 * f_dev, 1)
    pa0, pa1 = blk(pa_here, c, f_dev, 1), flip(blk(pa_here, 1 - c, f_dev, 1), "c")
    pa_got = flip(after(pa_there, *og_x), "xh")
    pa2, pa3 = blk(pa_got, c, f_dev, 1), flip(blk(pa_got, 1 - c, f_dev, 1), "c")
    pre_own = lay((pa0, pa1, pa2, pa3), 0, q)
    pre = ring_gather(pre_own, "y", y)

    wo_k, token = [], og_x
    for lo, hi in spans:
        got = flip(after(wo_there[:, lo:hi], *token), "xh")
        token = (got,)
        wo_k.append((
            jnp.concatenate([wo0[lo:hi], pick(got, c)], 1),
            jnp.concatenate([wo1[lo:hi], flip(pick(got, 1 - c), "c")], 1),
        ))
    wo_done = token

    og = ring_gather(og_blk, "z", z)
    og_o = flip(og, "c")

    hidden = []
    for (lo, hi), (wa, wb) in zip(spans, wo_k):
        part = dot_nt(og, wa) + dot_nt(og_o, wb)
        act_grad = ring_scatter(part.astype(BF), "y", y)
        own = (act_grad * gelu_slope(pre_own[:, lo:hi].astype(F32))).astype(BF)
        hidden.append(ring_gather(own, "y", y))

    li_x = x_parts(after(layer_input, *wo_done))
    li = ring_gather(x_join(layer_input, li_x, xl), "z", z)
    li_o = flip(li, "c")
    wi_here, wi_there = blk(w_in, xh, 2 * f_dev, 1), blk(w_in, 1 - xh, 2 * f_dev, 1)
    wi0, wi1 = blk(wi_here, c, f_dev, 1), flip(blk(wi_here, 1 - c, f_dev, 1), "c")
    wi_got = flip(after(wi_there, *wo_done, *li_x), "xh")
    wi2, wi3 = blk(wi_got, c, f_dev, 1), flip(blk(wi_got, 1 - c, f_dev, 1), "c")

    act = gelu_act(pre.astype(F32)).astype(BF)
    go, goo = dot_tn(act, og).astype(BF), dot_tn(act, og_o).astype(BF)
    far = jnp.concatenate([go[:, d_own:], goo[:, d_own:]], 1)
    w_out_grad = lay(unspread(go[:, :d_own], goo[:, :d_own], far, 1), 0, q)

    w_in_grad = jnp.zeros(w_in.shape, BF)
    for (lo, hi), h in zip(spans, hidden):
        gi, gio = dot_tn(li, h).astype(BF), dot_tn(li_o, h).astype(BF)
        far = jnp.concatenate([gi[d_own:], gio[d_own:]], 0)
        w_in_grad = lay(unspread(gi[:d_own], gio[:d_own], far, 0), 1, q, lo, w_in_grad)

    va, vb = jnp.concatenate([wi0, wi2], 0), jnp.concatenate([wi1, wi3], 0)
    (l0, h0), (l1, h1) = spans
    ig_o = dot_nt(hidden[0], vb[:, l0:h0]) + dot_nt(hidden[1], vb[:, l1:h1])
    ig = dot_nt(hidden[0], va[:, l0:h0]) + dot_nt(hidden[1], va[:, l1:h1])
    ig = ig + flip(ig_o.astype(BF), "c").astype(F32)
    ig = ring_scatter(ig.astype(BF), "z", z).astype(BF)
    near, other = blk(ig, xl, t_own, 0), blk(ig, 1 - xl, t_own, 0)
    input_grad = (
        near[:, :d_own].astype(F32)
        + flip(other[:, :d_own], "xl").astype(F32)
        + flip(near[:, d_own:], "xh").astype(F32)
        + flip(other[:, d_own:], "xl", "xh").astype(F32)
    ).astype(BF)

    b0 = jnp.concatenate([jnp.sum(h.astype(F32), axis=0) for h in hidden])
    b1 = flip(b0, "c")
    b23 = flip(jnp.stack([b0, b1]), "xh")
    bias_in = lay((b0, b1, b23[0], b23[1]), 0, q)
    bias_out = jnp.sum(og[:, :d_own].astype(F32), axis=0)
    return input_grad, w_in_grad, w_out_grad, bias_in, bias_out


def solution(mesh):
    fine = Mesh(mesh.devices.reshape(tuple(SIZES.values())), tuple(SIZES))
    row, col = ("z", "xl"), ("y", "xh", "c")
    in_specs = (P(row, col), P(row, col), P(col, row), P(col, row), P(row, col))
    out_specs = (P(row, col), P(col, row), P(row, col), P(row), P(col))
    return jax.shard_map(local, mesh=fine, in_specs=in_specs, out_specs=out_specs, check_vma=False)
```

```python
import jax
import jax.numpy as jnp
from jax import lax
from jax.sharding import Mesh, PartitionSpec as P

SIZES = {"z": 4, "xl": 2, "y": 4, "xh": 2, "c": 2}
BF, F32 = jnp.bfloat16, jnp.float32


def gelu_act(v):
    return v * (0.5 * (1.0 + lax.erf(v * 0.7071067811865476)))


def gelu_slope(v):
    normal_cdf = 0.5 * (1.0 + lax.erf(v * 0.7071067811865476))
    normal_pdf = jnp.exp(-0.5 * v * v) * 0.3989422804014327
    return normal_cdf + v * normal_pdf


def shift(x, axis, by):
    n = SIZES[axis]
    return lax.ppermute(x, axis, [(i, (i + by) % n) for i in range(n)])


def flip(x, *axes):
    n = 2 ** len(axes)
    return lax.ppermute(x, axes if len(axes) > 1 else axes[0], [(i, n - 1 - i) for i in range(n)])


def dot_nt(a, b):
    return lax.dot_general(a, b, (((1,), (1,)), ((), ())), preferred_element_type=F32)


def dot_tn(a, b):
    return lax.dot_general(a, b, (((0,), (0,)), ((), ())), preferred_element_type=F32)


def blk(x, i, size, axis):
    return lax.dynamic_slice_in_dim(x, i * size, size, axis)


def put(buf, x, i, axis):
    return lax.dynamic_update_slice_in_dim(buf, x, i * x.shape[axis], axis)


def after(x, *tokens):
    return lax.optimization_barrier((x, *tokens))[0]


def phase(tokens, *items):
    held = lax.optimization_barrier((*(x for _, x in items), *tokens))
    return [send(x) for (send, _), x in zip(items, held)]


def along(axis, by):
    return lambda x: shift(x, axis, by)


def over(*axes):
    return lambda x: flip(x, *axes)


def lay(parts, axis, q):
    shape = list(parts[0].shape)
    shape[axis] *= 4
    out = jnp.zeros(shape, parts[0].dtype)
    for d, part in enumerate(parts):
        out = put(out, part, q ^ d, axis)
    return out


def lay_ring(x, up, down, far, me):
    out = jnp.zeros((4 * x.shape[0], x.shape[1]), x.dtype)
    for k, part in ((0, x), (3, up), (1, down), (2, far)):
        out = put(out, part, (me + k) % 4, 0)
    return out


def ring_blocks(p, me):
    n = p.shape[0] // 4
    return [blk(p, (me + k) % 4, n, 0) for k in range(4)]


def x_join(g, gl, gh, gb, xl):
    first = xl == 0
    top = jnp.concatenate([jnp.where(first, g, gl), jnp.where(first, gh, gb)], 1)
    low = jnp.concatenate([jnp.where(first, gl, g), jnp.where(first, gb, gh)], 1)
    return jnp.concatenate([top, low], 0)


def pick(x, i):
    return lax.dynamic_index_in_dim(x, i, 0, keepdims=False)


def cat(*xs, axis=0):
    return jnp.concatenate(xs, axis)


def local(layer_input, out_grad, pre_act, w_in, w_out):
    z, xl, y, xh, c = (lax.axis_index(a) for a in ("z", "xl", "y", "xh", "c"))
    q = xh * 2 + c
    t_own, d_own = layer_input.shape
    f_dev = w_out.shape[0] // 4
    core, half = over("c"), lambda n: n // 2
    lo, hi = f_dev // 3, d_own // 3
    f32 = lambda x: x.astype(F32)

    li4 = lax.all_gather(layer_input, ("z", "xl", "xh"), axis=0).reshape(-1, 2, t_own, d_own)

    wo4 = w_out.reshape(2, 2, f_dev, d_own)
    wo_here, wo_there = pick(wo4, xh), pick(wo4, 1 - xh)
    pa_here, pa_there = blk(pre_act, xh, 2 * f_dev, 1), blk(pre_act, 1 - xh, 2 * f_dev, 1)
    gl, gh, gb, wo1, pa1 = tok = phase(
        (), (over("xl"), out_grad), (over("xh"), out_grad), (over("xl", "xh"), out_grad),
        (core, pick(wo_here, 1 - c)), (core, blk(pa_here, 1 - c, f_dev, 1)))
    og_blk = x_join(out_grad, gl, gh, gb, xl)

    pa_got, wo_a, og_up, og_dn, ogo_0 = tok = phase(
        tok, (over("xh"), pa_there), (over("xh"), wo_there[:, :lo]),
        (along("z", 1), og_blk), (along("z", -1), og_blk), (core, og_blk))
    pa = (blk(pa_here, c, f_dev, 1), pa1, blk(pa_got, c, f_dev, 1), core(blk(pa_got, 1 - c, f_dev, 1)))
    pre_own = lay(pa, 0, q)
    h = half(og_blk.shape[0])

    wo_b, og_fa, og_fb, pre_up, pre_dn = tok = phase(
        tok, (over("xh"), wo_there[:, lo:]), (along("z", 1), og_up[:h]), (along("z", -1), og_dn[h:]),
        (along("y", 1), pre_own), (along("y", -1), pre_own))
    og_far = cat(og_fa, og_fb)
    og = lay_ring(og_blk, og_up, og_dn, og_far, z)
    ogo_r = core(cat(og_up, og_dn))
    hp = half(pre_own.shape[0])

    n = og_blk.shape[0]
    wi_here, wi_there = blk(w_in, xh, 2 * f_dev, 1), blk(w_in, 1 - xh, 2 * f_dev, 1)
    wo3, ogo_f, pre_fa, pre_fb, wi_a = tok = phase(
        tok, (core, cat(pick(wo_a, 1 - c), pick(wo_b, 1 - c))), (core, og_far),
        (along("y", 1), pre_up[:hp]), (along("y", -1), pre_dn[hp:]), (over("xh"), wi_there[:hi]))
    og_o = lay_ring(ogo_0, ogo_r[:n], ogo_r[n:], ogo_f, z)
    wo2 = cat(pick(wo_a, c), pick(wo_b, c))
    part = dot_nt(og, cat(pick(wo_here, c), wo2, axis=1)) + dot_nt(og_o, cat(wo1, wo3, axis=1))
    b = ring_blocks(part.astype(BF), y)

    r1, l1, wi_b = tok = phase(
        tok, (along("y", 1), cat(b[2][:hp], b[1][hp:])), (along("y", -1), cat(b[3][:hp], b[2][hp:])),
        (over("xh"), wi_there[hi:]))
    pre = lay_ring(pre_own, pre_up, pre_dn, cat(pre_fa, pre_fb), y)
    act = gelu_act(f32(after(pre, b[0]))).astype(BF)
    go, goo = dot_tn(act, og).astype(BF), dot_tn(act, og_o).astype(BF)
    wog_far = cat(go[:, d_own:], goo[:, d_own:], axis=1)

    r2, l2, wog_a = tok = phase(
        tok, (along("y", 1), (f32(b[1][:hp]) + f32(r1[:hp])).astype(BF)),
        (along("y", -1), (f32(b[3][hp:]) + f32(l1[hp:])).astype(BF)), (over("xh"), wog_far[:lo]))
    act_grad = cat(f32(b[0][:hp]) + f32(l1[:hp]) + f32(r2), f32(b[0][hp:]) + f32(r1[hp:]) + f32(l2))
    h_own = (act_grad * gelu_slope(f32(pre_own))).astype(BF)

    h_up, h_dn, wog_b = tok = phase(
        tok, (along("y", 1), h_own), (along("y", -1), h_own), (over("xh"), wog_far[lo:]))
    wi_got = cat(wi_a, wi_b)
    wi1 = core(blk(wi_here, 1 - c, f_dev, 1))
    wi3 = core(blk(wi_got, 1 - c, f_dev, 1))
    va, vb = cat(blk(wi_here, c, f_dev, 1), blk(wi_got, c, f_dev, 1)), cat(wi1, wi3)
    lio4 = core(li4)
    side = lambda x, i: lax.dynamic_index_in_dim(x, i, 1, keepdims=False).reshape(-1, d_own)
    li_near, li_far = (cat(side(li4, i), side(lio4, i), axis=1) for i in (xh, 1 - xh))

    h_up, h_dn, wog_b = after((h_up, h_dn, wog_b))
    h_fa, h_fb = tok = phase((), (along("y", 1), h_up[:hp]), (along("y", -1), h_dn[hp:]))
    h_most, h_far = cat(h_own, h_up, h_dn), cat(h_fa, h_fb)
    hidden = lay_ring(h_own, h_up, h_dn, h_far, y)
    most_o, most = dot_nt(h_most, vb).astype(BF), dot_nt(h_most, va)
    far_o, far = dot_nt(h_far, vb).astype(BF), dot_nt(h_far, va)
    most = (most + f32(core(most_o))).astype(BF)
    far = (far + f32(core(far_o))).astype(BF)
    m = h_own.shape[0]
    ig = lay_ring(most[:m], most[m:2 * m], most[2 * m:], far, y)
    b = ring_blocks(ig, z)
    wig_far = dot_tn(li_far, hidden).astype(BF)

    r1, l1, wig_a = tok = phase(
        tok, (along("z", 1), cat(b[2][:h], b[1][h:])), (along("z", -1), cat(b[3][:h], b[2][h:])),
        (over("xh"), wig_far[:2 * lo]))
    wig_near = dot_tn(li_near, hidden).astype(BF)
    wog_got = cat(wog_a, wog_b)
    wog_rec = core(cat(goo[:, :d_own], wog_got[:, d_own:], axis=1))
    w_out_grad = lay((go[:, :d_own], wog_rec[:, :d_own], wog_got[:, :d_own], wog_rec[:, d_own:]), 0, q)

    r2, l2, wig_b = tok = phase(
        tok, (along("z", 1), (f32(b[1][:h]) + f32(r1[:h])).astype(BF)),
        (along("z", -1), (f32(b[3][h:]) + f32(l1[h:])).astype(BF)), (over("xh"), wig_far[2 * lo:]))
    ig = cat(f32(b[0][:h]) + f32(l1[:h]) + f32(r2), f32(b[0][h:]) + f32(r1[h:]) + f32(l2)).astype(BF)
    near, other = blk(ig, xl, t_own, 0), blk(ig, 1 - xl, t_own, 0)

    wig_got = cat(wig_a, wig_b)
    il, ih, ib, wig_rec = phase(
        tok, (over("xl"), other[:, :d_own]), (over("xh"), near[:, d_own:]), (over("xl", "xh"), other[:, d_own:]),
        (core, cat(wig_near[d_own:], wig_got[d_own:])))
    input_grad = (f32(near[:, :d_own]) + f32(il) + f32(ih) + f32(ib)).astype(BF)
    w_in_grad = lay((wig_near[:d_own], wig_rec[:d_own], wig_got[:d_own], wig_rec[d_own:]), 1, q)

    b0 = jnp.sum(f32(hidden), axis=0)
    b1 = core(b0)
    b23 = flip(jnp.stack([b0, b1]), "xh")
    bias_in = lay((b0, b1, b23[0], b23[1]), 0, q)
    bias_out = jnp.sum(f32(og[:, :d_own]), axis=0)
    return input_grad, w_in_grad, w_out_grad, bias_in, bias_out


def solution(mesh):
    fine = Mesh(mesh.devices.reshape(tuple(SIZES.values())), tuple(SIZES))
    row, col = ("z", "xl"), ("y", "xh", "c")
    in_specs = (P(row, col), P(row, col), P(col, row), P(col, row), P(row, col))
    out_specs = (P(row, col), P(col, row), P(row, col), P(row), P(col))
    return jax.shard_map(local, mesh=fine, in_specs=in_specs, out_specs=out_specs, check_vma=False)
```

```python
import jax
import jax.numpy as jnp
from jax import lax
from jax.sharding import Mesh, PartitionSpec as P

SIZES = {"z": 4, "xl": 2, "y": 4, "xh": 2, "c": 2}
BF, F32 = jnp.bfloat16, jnp.float32


def gelu_act(v):
    return v * (0.5 * (1.0 + lax.erf(v * 0.7071067811865476)))


def gelu_slope(v):
    normal_cdf = 0.5 * (1.0 + lax.erf(v * 0.7071067811865476))
    normal_pdf = jnp.exp(-0.5 * v * v) * 0.3989422804014327
    return normal_cdf + v * normal_pdf


def shift(x, axis, by):
    n = SIZES[axis]
    return lax.ppermute(x, axis, [(i, (i + by) % n) for i in range(n)])


def flip(x, *axes):
    n = 2 ** len(axes)
    return lax.ppermute(x, axes if len(axes) > 1 else axes[0], [(i, n - 1 - i) for i in range(n)])


def dot_nt(a, b):
    return lax.dot_general(a, b, (((1,), (1,)), ((), ())), preferred_element_type=F32)


def dot_tn(a, b):
    return lax.dot_general(a, b, (((0,), (0,)), ((), ())), preferred_element_type=F32)


def blk(x, i, size, axis):
    return lax.dynamic_slice_in_dim(x, i * size, size, axis)


def put(buf, x, i, axis):
    return lax.dynamic_update_slice_in_dim(buf, x, i * x.shape[axis], axis)


def hold(*xs):
    return lax.optimization_barrier(xs)


def phase(tokens, *items):
    held = hold(*(x for _, x in items), *tokens)
    return [send(x) for (send, _), x in zip(items, held)]


def along(axis, by):
    return lambda x: shift(x, axis, by)


def over(*axes):
    return lambda x: flip(x, *axes)


def lay(parts, axis, q):
    shape = list(parts[0].shape)
    shape[axis] *= 4
    out = jnp.zeros(shape, parts[0].dtype)
    for d, part in enumerate(parts):
        out = put(out, part, q ^ d, axis)
    return out


def lay_ring(x, up, down, far, me):
    out = jnp.zeros((4 * x.shape[0], x.shape[1]), x.dtype)
    for k, part in ((0, x), (3, up), (1, down), (2, far)):
        out = put(out, part, (me + k) % 4, 0)
    return out


def ring_blocks(p, me):
    n = p.shape[0] // 4
    return [blk(p, (me + k) % 4, n, 0) for k in range(4)]


def x_join(g, gl, gh, gb, xl):
    first = xl == 0
    top = jnp.concatenate([jnp.where(first, g, gl), jnp.where(first, gh, gb)], 1)
    low = jnp.concatenate([jnp.where(first, gl, g), jnp.where(first, gb, gh)], 1)
    return jnp.concatenate([top, low], 0)


def pick(x, i):
    return lax.dynamic_index_in_dim(x, i, 0, keepdims=False)


def cat(*xs, axis=0):
    return jnp.concatenate(xs, axis)


def local(layer_input, out_grad, pre_act, w_in, w_out):
    z, xl, y, xh, c = (lax.axis_index(a) for a in ("z", "xl", "y", "xh", "c"))
    q = xh * 2 + c
    t_own, d_own = layer_input.shape
    f_dev = w_out.shape[0] // 4
    core, cross = over("c"), over("xh")
    lo, hi = f_dev // 3, d_own // 3
    f32 = lambda x: x.astype(F32)
    up, down = {a: along(a, 1) for a in "yz"}, {a: along(a, -1) for a in "yz"}

    gl, gh, gb = cross_x = over("xl")(out_grad), cross(out_grad), over("xl", "xh")(out_grad)
    wo4 = w_out.reshape(2, 2, f_dev, d_own)
    wo_here, wo_there = pick(wo4, xh), pick(wo4, 1 - xh)
    pa_here, pa_there = blk(pre_act, xh, 2 * f_dev, 1), blk(pre_act, 1 - xh, 2 * f_dev, 1)
    wo0, wo1 = pick(wo_here, c), core(pick(wo_here, 1 - c))
    pa1 = core(blk(pa_here, 1 - c, f_dev, 1))
    g0 = x_join(out_grad, gl, gh, gb, xl)

    g3, g1, pa_got, wo_a = tok = phase(
        cross_x, (up["z"], g0), (down["z"], g0), (cross, pa_there), (cross, wo_there[:, :lo]))
    go0 = core(g0)
    pa = (blk(pa_here, c, f_dev, 1), pa1, blk(pa_got, c, f_dev, 1), core(blk(pa_got, 1 - c, f_dev, 1)))
    pre_own = lay(pa, 0, q)
    h, hp = g0.shape[0] // 2, pre_own.shape[0] // 2

    pre_up, pre_dn, g2a, g2b, wo_b = tok = phase(
        tok, (up["y"], pre_own), (down["y"], pre_own), (up["z"], g3[:h]), (down["z"], g1[h:]),
        (cross, wo_there[:, lo:]))
    go3, go1 = core(g3), core(g1)
    wi_here, wi_there = blk(w_in, xh, 2 * f_dev, 1), blk(w_in, 1 - xh, 2 * f_dev, 1)

    pre_up, pre_dn, g2a, g2b, wo_a, wo_b = hold(pre_up, pre_dn, g2a, g2b, wo_a, wo_b)
    pre_fa, pre_fb = up["y"](pre_up[:hp]), down["y"](pre_dn[hp:])
    wi_a, ll = cross(hold(wi_there[:hi], g2a)[0]), over("xl")(hold(layer_input, g2a)[0])
    tok = pre_fa, pre_fb, wi_a, ll
    wo3 = core(cat(pick(wo_a, 1 - c), pick(wo_b, 1 - c)))
    g2 = cat(g2a, g2b)
    go2 = core(g2)
    k_own, k_oth = cat(wo0, cat(pick(wo_a, c), pick(wo_b, c)), axis=1), cat(wo1, wo3, axis=1)
    part = [(dot_nt(g, k_own) + dot_nt(o, k_oth)).astype(BF) for g, o in ((g0, go0), (g3, go3), (g1, go1), (g2, go2))]
    part = lay_ring(part[0], part[1], part[2], part[3], z)
    b = ring_blocks(part, y)

    first = xl == 0
    l_rows = cat(jnp.where(first, layer_input, ll), jnp.where(first, ll, layer_input))
    r1, l1, wi_b, lh = tok = phase(
        tok, (up["y"], cat(b[2][:hp], b[1][hp:])), (down["y"], cat(b[3][:hp], b[2][hp:])),
        (cross, wi_there[hi:2 * hi]), (cross, l_rows))
    pre_fa, pre_fb, part = hold(pre_fa, pre_fb, part)
    og, og_o = lay_ring(g0, g3, g1, g2, z), lay_ring(go0, go3, go1, go2, z)
    pre = lay_ring(pre_own, pre_up, pre_dn, cat(pre_fa, pre_fb), y)
    act = gelu_act(f32(pre)).astype(BF)
    go, goo = dot_tn(act, og).astype(BF), dot_tn(act, og_o).astype(BF)
    wog_far = cat(go[:, d_own:], goo[:, d_own:], axis=1)

    r2, l2, wi_c = tok = phase(
        tok, (up["y"], (f32(b[1][:hp]) + f32(r1[:hp])).astype(BF)),
        (down["y"], (f32(b[3][hp:]) + f32(l1[hp:])).astype(BF)), (cross, wi_there[2 * hi:]))
    slope, part = hold(gelu_slope(f32(pre_own)), part)
    act_grad = cat(f32(b[0][:hp]) + f32(l1[:hp]) + f32(r2), f32(b[0][hp:]) + f32(r1[hp:]) + f32(l2))
    h0 = (act_grad * slope).astype(BF)
    li0 = cat(l_rows, lh, axis=1)

    h3, h1, li3, li1, wog_a = tok = phase(
        tok, (up["y"], h0), (down["y"], h0), (up["z"], li0), (down["z"], li0), (cross, wog_far[:2 * lo]))
    wi_got = cat(wi_a, wi_b, wi_c)
    va = cat(blk(wi_here, c, f_dev, 1), blk(wi_got, c, f_dev, 1))
    vb = cat(core(blk(wi_here, 1 - c, f_dev, 1)), core(blk(wi_got, 1 - c, f_dev, 1)))
    lio0 = core(li0)

    def ig_block(h_k):
        other = core(dot_nt(h_k, vb).astype(BF))
        return (dot_nt(h_k, va) + f32(other)).astype(BF)

    h3, h1, li3, li1, wog_a = hold(h3, h1, li3, li1, wog_a)
    h2a, h2b, li2a, li2b, wog_b = tok = (
        up["y"](h3[:hp]), down["y"](h1[hp:]), up["z"](li3[:h]), down["z"](li1[h:]), cross(hold(wog_far[2 * lo:], h3)[0]))
    most = ig_block(cat(h0, h3, h1))
    lio3, lio1 = core(li3), core(li1)
    h2a, h2b, li2a, li2b, wog_b = hold(*tok)
    h2, li2 = cat(h2a, h2b), cat(li2a, li2b)
    m = h0.shape[0]
    far = ig_block(h2)
    b = ring_blocks(lay_ring(most[:m], most[m:2 * m], most[2 * m:], far, y), z)

    r1, l1 = up["z"](cat(b[2][:h], b[1][h:])), down["z"](cat(b[3][:h], b[2][h:]))
    lio2 = core(li2)
    hidden = lay_ring(h0, h3, h1, h2, y)
    li, li_o = lay_ring(li0, li3, li1, li2, z), lay_ring(lio0, lio3, lio1, lio2, z)
    gi, gio = dot_tn(li, hidden).astype(BF), dot_tn(li_o, hidden).astype(BF)
    wig_far = cat(gi[d_own:], gio[d_own:])
    wig_a = cross(wig_far[:2 * lo])
    b0 = jnp.sum(f32(hidden), axis=0)
    b1 = core(b0)
    b23 = cross(jnp.stack([b0, b1]))
    wog_got = cat(wog_a, wog_b)
    wog_rec = core(cat(goo[:, :d_own], wog_got[:, d_own:], axis=1))
    w_out_grad = lay((go[:, :d_own], wog_rec[:, :d_own], wog_got[:, :d_own], wog_rec[:, d_own:]), 0, q)
    bias_in = lay((b0, b1, b23[0], b23[1]), 0, q)
    bias_out = jnp.sum(f32(og[:, :d_own]), axis=0)

    r2, l2, wig_b = tok = phase(
        (r1, l1, wig_a, b23, wog_rec), (up["z"], (f32(b[1][:h]) + f32(r1[:h])).astype(BF)),
        (down["z"], (f32(b[3][h:]) + f32(l1[h:])).astype(BF)), (cross, wig_far[2 * lo:]))
    ig = cat(f32(b[0][:h]) + f32(l1[:h]) + f32(r2), f32(b[0][h:]) + f32(r1[h:]) + f32(l2)).astype(BF)
    near, other = blk(ig, xl, t_own, 0), blk(ig, 1 - xl, t_own, 0)

    il, ih, ib = over("xl")(other[:, :d_own]), cross(near[:, d_own:]), over("xl", "xh")(other[:, d_own:])
    wig_got = cat(wig_a, wig_b)
    wig_rec = core(hold(cat(gio[:d_own], wig_got[d_own:]), near)[0])
    input_grad = (f32(near[:, :d_own]) + f32(il) + f32(ih) + f32(ib)).astype(BF)
    w_in_grad = lay((gi[:d_own], wig_rec[:d_own], wig_got[:d_own], wig_rec[d_own:]), 1, q)
    return input_grad, w_in_grad, w_out_grad, bias_in, bias_out


def solution(mesh):
    fine = Mesh(mesh.devices.reshape(tuple(SIZES.values())), tuple(SIZES))
    row, col = ("z", "xl"), ("y", "xh", "c")
    in_specs = (P(row, col), P(row, col), P(col, row), P(col, row), P(row, col))
    out_specs = (P(row, col), P(col, row), P(row, col), P(row), P(col))
    return jax.shard_map(local, mesh=fine, in_specs=in_specs, out_specs=out_specs, check_vma=False)
```

```python
import jax
import jax.numpy as jnp
from jax import lax
from jax.sharding import Mesh, PartitionSpec as P

SIZES = {"z": 4, "xl": 2, "y": 4, "xh": 2, "c": 2}
BF, F32 = jnp.bfloat16, jnp.float32


def gelu_act(v):
    return v * (0.5 * (1.0 + lax.erf(v * 0.7071067811865476)))


def gelu_slope(v):
    normal_cdf = 0.5 * (1.0 + lax.erf(v * 0.7071067811865476))
    normal_pdf = jnp.exp(-0.5 * v * v) * 0.3989422804014327
    return normal_cdf + v * normal_pdf


def shift(x, axis, by):
    n = SIZES[axis]
    return lax.ppermute(x, axis, [(i, (i + by) % n) for i in range(n)])


def flip(x, *axes):
    n = 2 ** len(axes)
    return lax.ppermute(x, axes if len(axes) > 1 else axes[0], [(i, n - 1 - i) for i in range(n)])


def dot_nt(a, b):
    return lax.dot_general(a, b, (((1,), (1,)), ((), ())), preferred_element_type=F32)


def dot_tn(a, b):
    return lax.dot_general(a, b, (((0,), (0,)), ((), ())), preferred_element_type=F32)


def blk(x, i, size, axis):
    return lax.dynamic_slice_in_dim(x, i * size, size, axis)


def put(buf, x, i, axis):
    return lax.dynamic_update_slice_in_dim(buf, x, i * x.shape[axis], axis)


def hold(*xs):
    return lax.optimization_barrier(xs)


def phase(tokens, *items):
    held = hold(*(x for _, x in items), *tokens)
    return [send(x) for (send, _), x in zip(items, held)]


def along(axis, by):
    return lambda x: shift(x, axis, by)


def both_ways(axis, a, b):
    a, b = hold(a, b)
    return hold(shift(a, axis, 1), shift(b, axis, -1))


def over(*axes):
    return lambda x: flip(x, *axes)


def lay(parts, axis, q):
    shape = list(parts[0].shape)
    shape[axis] *= 4
    out = jnp.zeros(shape, parts[0].dtype)
    for d, part in enumerate(parts):
        out = put(out, part, q ^ d, axis)
    return out


def lay_ring(x, up, down, far, me):
    out = jnp.zeros((4 * x.shape[0], x.shape[1]), x.dtype)
    for k, part in ((0, x), (3, up), (1, down), (2, far)):
        out = put(out, part, (me + k) % 4, 0)
    return out


def ring_blocks(p, me):
    n = p.shape[0] // 4
    return [blk(p, (me + k) % 4, n, 0) for k in range(4)]


def x_join(g, gl, gh, gb, xl):
    first = xl == 0
    top = jnp.concatenate([jnp.where(first, g, gl), jnp.where(first, gh, gb)], 1)
    low = jnp.concatenate([jnp.where(first, gl, g), jnp.where(first, gb, gh)], 1)
    return jnp.concatenate([top, low], 0)


def pick(x, i):
    return lax.dynamic_index_in_dim(x, i, 0, keepdims=False)


def cat(*xs, axis=0):
    return jnp.concatenate(xs, axis)


def local(layer_input, out_grad, pre_act, w_in, w_out):
    z, xl, y, xh, c = (lax.axis_index(a) for a in ("z", "xl", "y", "xh", "c"))
    q = xh * 2 + c
    t_own, d_own = layer_input.shape
    f_dev = w_out.shape[0] // 4
    core, cross = over("c"), over("xh")
    f32 = lambda x: x.astype(F32)
    up, down = {a: along(a, 1) for a in "yz"}, {a: along(a, -1) for a in "yz"}

    gl, gh, gb = cross_x = over("xl")(out_grad), cross(out_grad), over("xl", "xh")(out_grad)
    wo4 = w_out.reshape(2, 2, f_dev, d_own)
    wo_here, wo_there = pick(wo4, xh), pick(wo4, 1 - xh)
    pa_here, pa_there = blk(pre_act, xh, 2 * f_dev, 1), blk(pre_act, 1 - xh, 2 * f_dev, 1)
    wo0, wo1 = pick(wo_here, c), core(pick(wo_here, 1 - c))
    pa1 = core(blk(pa_here, 1 - c, f_dev, 1))
    g0 = x_join(out_grad, gl, gh, gb, xl)

    g3, g1, pa_got, wo_got = phase(cross_x, (up["z"], g0), (down["z"], g0), (cross, pa_there), (cross, wo_there))
    g3, g1, pa_got = hold(g3, g1, pa_got)
    pa = (blk(pa_here, c, f_dev, 1), pa1, blk(pa_got, c, f_dev, 1), core(blk(pa_got, 1 - c, f_dev, 1)))
    pre_own = lay(pa, 0, q)
    pre = lax.all_gather(pre_own, "y", axis=0, tiled=True)
    h, hp = g0.shape[0] // 2, pre_own.shape[0] // 2
    g2a, g2b = both_ways("z", g3[:h], g1[h:])
    og = lay_ring(g0, g3, g1, cat(g2a, g2b), z)
    og, wo_got = hold(og, wo_got)
    og_o = core(og)
    wo3 = core(pick(wo_got, 1 - c))

    mine = hold(dot_nt(og, cat(wo0, pick(wo_got, c), axis=1)), og)[0]
    part = (mine + dot_nt(og_o, cat(wo1, wo3, axis=1))).astype(BF)
    b = ring_blocks(part, y)

    wi_here, wi_there = blk(w_in, xh, 2 * f_dev, 1), blk(w_in, 1 - xh, 2 * f_dev, 1)
    r1, l1 = both_ways("y", cat(b[2][:hp], b[1][hp:]), cat(b[3][:hp], b[2][hp:]))
    wi_got = cross(hold(wi_there, og_o)[0])
    li = lax.all_gather(hold(layer_input, g2a, g2b)[0], ("xh", "c", "z", "xl"), axis=0)
    act = gelu_act(f32(hold(pre, part)[0])).astype(BF)
    go, goo = dot_tn(act, og).astype(BF), dot_tn(act, og_o).astype(BF)
    wog_far = cat(go[:, d_own:], goo[:, d_own:], axis=1)
    r1, l1, go = hold(r1, l1, go)
    r2, l2 = both_ways("y", (f32(b[1][:hp]) + f32(r1[:hp])).astype(BF), (f32(b[3][hp:]) + f32(l1[hp:])).astype(BF))
    slope = hold(gelu_slope(f32(pre_own)), l1)[0]
    act_grad = cat(f32(b[0][:hp]) + f32(l1[:hp]) + f32(r2), f32(b[0][hp:]) + f32(r1[hp:]) + f32(l2))
    h0 = (act_grad * slope).astype(BF)

    wi1, wi3 = core(blk(wi_here, 1 - c, f_dev, 1)), core(blk(wi_got, 1 - c, f_dev, 1))
    va, vb = cat(blk(wi_here, c, f_dev, 1), blk(wi_got, c, f_dev, 1)), cat(wi1, wi3)
    va, vb = hold(va, vb)

    def ig_block(h_k):
        other = core(dot_nt(h_k, vb).astype(BF))
        return (dot_nt(h_k, va) + f32(other)).astype(BF)

    h3, h1, wog_got = tok = phase((wi_got,), (up["y"], h0), (down["y"], h0), (cross, wog_far))
    own = ig_block(h0)
    h3, h1 = hold(h3, h1)
    h2a, h2b = both_ways("y", h3[:hp], h1[hp:])
    most = ig_block(cat(h3, h1))
    h2a, h2b, wog_got, own = hold(h2a, h2b, wog_got, own)
    h2 = cat(h2a, h2b)
    m = h0.shape[0]
    b = ring_blocks(lay_ring(own, most[:m], most[m:], ig_block(h2), y), z)
    first_up, first_dn = cat(b[2][:h], b[1][h:]), cat(b[3][:h], b[2][h:])

    first_up, first_dn = hold(first_up, first_dn)
    r1, l1 = up["z"](first_up), down["z"](first_dn)
    hidden = hold(lay_ring(h0, h3, h1, h2, y), first_up, first_dn)[0]
    li4 = li.reshape(4, -1, d_own)
    gi = [dot_tn(pick(li4, q ^ d), hidden).astype(BF) for d in range(4)]
    wig_got = cross(cat(gi[2], gi[3]))
    wog_rec = core(cat(goo[:, :d_own], wog_got[:, d_own:], axis=1))
    w_out_grad = lay((go[:, :d_own], wog_rec[:, :d_own], wog_got[:, :d_own], wog_rec[:, d_own:]), 0, q)
    b0 = jnp.sum(f32(hidden), axis=0)
    b1 = core(b0)
    b23 = cross(jnp.stack([b0, b1]))
    bias_in = lay((b0, b1, b23[0], b23[1]), 0, q)
    bias_out = jnp.sum(f32(og[:, :d_own]), axis=0)
    w1 = core(gi[1])

    r1, l1, b23, wog_rec, w1 = hold(r1, l1, b23, wog_rec, w1)
    r2, l2 = both_ways("z", (f32(b[1][:h]) + f32(r1[:h])).astype(BF), (f32(b[3][h:]) + f32(l1[h:])).astype(BF))
    ig = cat(f32(b[0][:h]) + f32(l1[:h]) + f32(r2), f32(b[0][h:]) + f32(r1[h:]) + f32(l2)).astype(BF)
    near, other = blk(ig, xl, t_own, 0), blk(ig, 1 - xl, t_own, 0)

    il, ih, ib = over("xl")(other[:, :d_own]), cross(near[:, d_own:]), over("xl", "xh")(other[:, d_own:])
    w3 = core(wig_got[d_own:])
    input_grad = (f32(near[:, :d_own]) + f32(il) + f32(ih) + f32(ib)).astype(BF)
    w_in_grad = lay((gi[0], w1, wig_got[:d_own], w3), 1, q)
    return input_grad, w_in_grad, w_out_grad, bias_in, bias_out


def solution(mesh):
    fine = Mesh(mesh.devices.reshape(tuple(SIZES.values())), tuple(SIZES))
    row, col = ("z", "xl"), ("y", "xh", "c")
    in_specs = (P(row, col), P(row, col), P(col, row), P(col, row), P(row, col))
    out_specs = (P(row, col), P(col, row), P(row, col), P(row), P(col))
    return jax.shard_map(local, mesh=fine, in_specs=in_specs, out_specs=out_specs, check_vma=False)
```

```python
import jax
import jax.numpy as jnp
from jax import lax
from jax.sharding import Mesh, PartitionSpec as P

SIZES = {"z": 4, "xl": 2, "y": 4, "xh": 2, "c": 2}
BF, F32 = jnp.bfloat16, jnp.float32


def gelu_act(v):
    return v * (0.5 * (1.0 + lax.erf(v * 0.7071067811865476)))


def gelu_slope(v):
    normal_cdf = 0.5 * (1.0 + lax.erf(v * 0.7071067811865476))
    normal_pdf = jnp.exp(-0.5 * v * v) * 0.3989422804014327
    return normal_cdf + v * normal_pdf


def shift(x, axis, by):
    n = SIZES[axis]
    return lax.ppermute(x, axis, [(i, (i + by) % n) for i in range(n)])


def flip(x, *axes):
    n = 2 ** len(axes)
    return lax.ppermute(x, axes if len(axes) > 1 else axes[0], [(i, n - 1 - i) for i in range(n)])


def dot_nt(a, b):
    return lax.dot_general(a, b, (((1,), (1,)), ((), ())), preferred_element_type=F32)


def dot_tn(a, b):
    return lax.dot_general(a, b, (((0,), (0,)), ((), ())), preferred_element_type=F32)


def blk(x, i, size, axis):
    return lax.dynamic_slice_in_dim(x, i * size, size, axis)


def put(buf, x, i, axis):
    return lax.dynamic_update_slice_in_dim(buf, x, i * x.shape[axis], axis)


def hold(*xs):
    return lax.optimization_barrier(xs)


def phase(tokens, *items):
    held = hold(*(x for _, x in items), *tokens)
    return [send(x) for (send, _), x in zip(items, held)]


def along(axis, by):
    return lambda x: shift(x, axis, by)


def both_ways(axis, a, b):
    a, b = hold(a, b)
    return hold(shift(a, axis, 1), shift(b, axis, -1))


def over(*axes):
    return lambda x: flip(x, *axes)


def lay(parts, axis, q):
    shape = list(parts[0].shape)
    shape[axis] *= 4
    out = jnp.zeros(shape, parts[0].dtype)
    for d, part in enumerate(parts):
        out = put(out, part, q ^ d, axis)
    return out


def lay_ring(x, up, down, far, me):
    out = jnp.zeros((4 * x.shape[0], x.shape[1]), x.dtype)
    for k, part in ((0, x), (3, up), (1, down), (2, far)):
        out = put(out, part, (me + k) % 4, 0)
    return out


def ring_blocks(p, me):
    n = p.shape[0] // 4
    return [blk(p, (me + k) % 4, n, 0) for k in range(4)]


def x_join(g, gl, gh, gb, xl):
    first = xl == 0
    top = jnp.concatenate([jnp.where(first, g, gl), jnp.where(first, gh, gb)], 1)
    low = jnp.concatenate([jnp.where(first, gl, g), jnp.where(first, gb, gh)], 1)
    return jnp.concatenate([top, low], 0)


def pick(x, i):
    return lax.dynamic_index_in_dim(x, i, 0, keepdims=False)


def cat(*xs, axis=0):
    return jnp.concatenate(xs, axis)


def local(layer_input, out_grad, pre_act, w_in, w_out):
    z, xl, y, xh, c = (lax.axis_index(a) for a in ("z", "xl", "y", "xh", "c"))
    q = xh * 2 + c
    t_own, d_own = layer_input.shape
    f_dev = w_out.shape[0] // 4
    core, cross = over("c"), over("xh")
    f32 = lambda x: x.astype(F32)
    up, down = {a: along(a, 1) for a in "yz"}, {a: along(a, -1) for a in "yz"}

    gl, gh, gb = over("xl")(out_grad), cross(out_grad), over("xl", "xh")(out_grad)
    wo4 = w_out.reshape(2, 2, f_dev, d_own)
    wo_here, wo_there = pick(wo4, xh), pick(wo4, 1 - xh)
    pa_here, pa_there = blk(pre_act, xh, 2 * f_dev, 1), blk(pre_act, 1 - xh, 2 * f_dev, 1)
    wo0, wo1 = pick(wo_here, c), core(pick(wo_here, 1 - c))
    pa1 = core(blk(pa_here, 1 - c, f_dev, 1))
    g0 = x_join(out_grad, gl, gh, gb, xl)
    h, hp, hf = g0.shape[0] // 2, 2 * pre_act.shape[0], f_dev // 2

    g0, pa_there, wo_op = hold(g0, pa_there, wo_there[:, :hf])
    g3, g1, pa_got, wo_a = hold(up["z"](g0), down["z"](g0), cross(pa_there), cross(wo_op))
    pa = (blk(pa_here, c, f_dev, 1), pa1, blk(pa_got, c, f_dev, 1), core(blk(pa_got, 1 - c, f_dev, 1)))
    pre_own = lay(pa, 0, q)
    pre_up, pre_dn = up["y"](pre_own), down["y"](pre_own)
    slope = gelu_slope(f32(pre_own))

    op_a, op_b, wo_op = hold(g3[:h], g1[h:], wo_there[:, hf:])
    g2a, g2b, wo_b, slope = hold(up["z"](op_a), down["z"](op_b), cross(wo_op), slope)
    og = lay_ring(g0, g3, g1, cat(g2a, g2b), z)
    og_o = core(og)
    wo3 = core(cat(pick(wo_a, 1 - c), pick(wo_b, 1 - c)))
    wo2 = cat(pick(wo_a, c), pick(wo_b, c))

    part = (dot_nt(og, cat(wo0, wo2, axis=1)) + dot_nt(og_o, cat(wo1, wo3, axis=1))).astype(BF)
    b = ring_blocks(part, y)
    wi_here, wi_there = blk(w_in, xh, 2 * f_dev, 1), blk(w_in, 1 - xh, 2 * f_dev, 1)
    op_a, op_b, wi_there, l_in, pre_up, pre_dn = hold(
        cat(b[2][:hp], b[1][hp:]), cat(b[3][:hp], b[2][hp:]), wi_there, layer_input, pre_up, pre_dn)
    r1, l1, wi_got, ll = up["y"](op_a), down["y"](op_b), cross(wi_there), over("xl")(l_in)
    pre_fa, pre_fb = up["y"](pre_up[:hp]), down["y"](pre_dn[hp:])
    r1, l1, ll, pre_fa, pre_fb = hold(r1, l1, ll, pre_fa, pre_fb)
    first = xl == 0
    l_rows = cat(jnp.where(first, layer_input, ll), jnp.where(first, ll, layer_input))
    op_a, op_b, l_rows, pre_fa = hold(
        (f32(b[1][:hp]) + f32(r1[:hp])).astype(BF), (f32(b[3][hp:]) + f32(l1[hp:])).astype(BF), l_rows, pre_fa)
    r2, l2, lh = up["y"](op_a), down["y"](op_b), cross(l_rows)
    pre = lay_ring(pre_own, pre_up, pre_dn, cat(pre_fa, pre_fb), y)
    act = gelu_act(f32(pre)).astype(BF)
    go = dot_tn(act, og).astype(BF)
    r2, l2, lh, go = hold(r2, l2, lh, go)
    act_grad = cat(f32(b[0][:hp]) + f32(l1[:hp]) + f32(r2), f32(b[0][hp:]) + f32(r1[hp:]) + f32(l2))
    h0 = (act_grad * slope).astype(BF)

    h0, li0, act, wi_got = hold(h0, cat(l_rows, lh, axis=1), act, wi_got)
    h3, h1, li3, li1 = up["y"](h0), down["y"](h0), up["z"](li0), down["z"](li0)
    goo = dot_tn(act, og_o).astype(BF)
    wog_got = cross(cat(go[:, d_own:], goo[:, d_own:], axis=1))
    wi1, wi3 = core(blk(wi_here, 1 - c, f_dev, 1)), core(blk(wi_got, 1 - c, f_dev, 1))
    va, vb = cat(blk(wi_here, c, f_dev, 1), blk(wi_got, c, f_dev, 1)), cat(wi1, wi3)

    def ig_block(h_k):
        other = core(dot_nt(h_k, vb).astype(BF))
        return (dot_nt(h_k, va) + f32(other)).astype(BF)

    h3, h1, li3, li1, va, vb = hold(h3, h1, li3, li1, va, vb)
    op_a, op_b, op_c, op_d, h0, h31 = hold(h3[:hp], h1[hp:], li3[:h], li1[h:], h0, cat(h3, h1))
    h2a, h2b, li2a, li2b = up["y"](op_a), down["y"](op_b), up["z"](op_c), down["z"](op_d)
    own, most = ig_block(h0), ig_block(h31)
    h2a, h2b, own, most = hold(h2a, h2b, own, most)
    h2 = cat(h2a, h2b)
    m = h0.shape[0]
    b = ring_blocks(lay_ring(own, most[:m], most[m:], ig_block(h2), y), z)

    op_a, op_b, h2, goo, wog_got, li2a, li2b, og = hold(
        cat(b[2][:h], b[1][h:]), cat(b[3][:h], b[2][h:]), h2, goo, wog_got, li2a, li2b, og)
    r1, l1 = up["z"](op_a), down["z"](op_b)
    li = lay_ring(li0, li3, li1, cat(li2a, li2b), z)
    li_o = core(li)
    hidden = lay_ring(h0, h3, h1, h2, y)
    gi, gio = dot_tn(li, hidden).astype(BF), dot_tn(li_o, hidden).astype(BF)
    wig_far = cat(gi[d_own:], gio[d_own:])
    wig_got = cross(wig_far)
    wog_rec = core(cat(goo[:, :d_own], wog_got[:, d_own:], axis=1))
    b0 = jnp.sum(f32(hidden), axis=0)
    b1 = core(b0)
    b23 = cross(jnp.stack([b0, b1]))

    r1, l1, b23, wog_rec, gi, wig_far = hold(r1, l1, b23, wog_rec, gi, wig_far)
    op_a, op_b, wog_rec, b23, og, gio, wig_far = hold(
        (f32(b[1][:h]) + f32(r1[:h])).astype(BF), (f32(b[3][h:]) + f32(l1[h:])).astype(BF), wog_rec, b23, og, gio, wig_far)
    r2, l2 = up["z"](op_a), down["z"](op_b)
    w1 = core(gio[:d_own])
    w_out_grad = lay((go[:, :d_own], wog_rec[:, :d_own], wog_got[:, :d_own], wog_rec[:, d_own:]), 0, q)
    bias_in = lay((b0, b1, b23[0], b23[1]), 0, q)
    bias_out = jnp.sum(f32(og[:, :d_own]), axis=0)
    r2, l2, w1, w_out_grad = hold(r2, l2, w1, w_out_grad)
    ig = cat(f32(b[0][:h]) + f32(l1[:h]) + f32(r2), f32(b[0][h:]) + f32(r1[h:]) + f32(l2)).astype(BF)
    near, other = blk(ig, xl, t_own, 0), blk(ig, 1 - xl, t_own, 0)

    op_a, op_b, op_c, wig_got, gi = hold(other[:, :d_own], near[:, d_own:], other[:, d_own:], wig_got, gi)
    il, ih, ib = over("xl")(op_a), cross(op_b), over("xl", "xh")(op_c)
    w3 = core(wig_got[d_own:])
    input_grad = (f32(near[:, :d_own]) + f32(il) + f32(ih) + f32(ib)).astype(BF)
    w_in_grad = lay((gi[:d_own], w1, wig_got[:d_own], w3), 1, q)
    return input_grad, w_in_grad, w_out_grad, bias_in, bias_out


def solution(mesh):
    fine = Mesh(mesh.devices.reshape(tuple(SIZES.values())), tuple(SIZES))
    row, col = ("z", "xl"), ("y", "xh", "c")
    in_specs = (P(row, col), P(row, col), P(col, row), P(col, row), P(row, col))
    out_specs = (P(row, col), P(col, row), P(row, col), P(row), P(col))
    return jax.shard_map(local, mesh=fine, in_specs=in_specs, out_specs=out_specs, check_vma=False)
```

```python
import jax
import jax.numpy as jnp
from jax import lax
from jax.sharding import Mesh, PartitionSpec as P

SIZES = {"z": 4, "xl": 2, "y": 4, "xh": 2, "c": 2}
BF, F32 = jnp.bfloat16, jnp.float32


def gelu_act(v):
    return v * (0.5 * (1.0 + lax.erf(v * 0.7071067811865476)))


def gelu_slope(v):
    normal_cdf = 0.5 * (1.0 + lax.erf(v * 0.7071067811865476))
    normal_pdf = jnp.exp(-0.5 * v * v) * 0.3989422804014327
    return normal_cdf + v * normal_pdf


def shift(x, axis, by):
    n = SIZES[axis]
    return lax.ppermute(x, axis, [(i, (i + by) % n) for i in range(n)])


def flip(x, *axes):
    n = 2 ** len(axes)
    return lax.ppermute(x, axes if len(axes) > 1 else axes[0], [(i, n - 1 - i) for i in range(n)])


def dot_nt(a, b):
    return lax.dot_general(a, b, (((1,), (1,)), ((), ())), preferred_element_type=F32)


def dot_tn(a, b):
    return lax.dot_general(a, b, (((0,), (0,)), ((), ())), preferred_element_type=F32)


def blk(x, i, size, axis):
    return lax.dynamic_slice_in_dim(x, i * size, size, axis)


def put(buf, x, i, axis):
    return lax.dynamic_update_slice_in_dim(buf, x, i * x.shape[axis], axis)


def hold(*xs):
    return lax.optimization_barrier(xs)


def phase(tokens, *items):
    held = hold(*(x for _, x in items), *tokens)
    return [send(x) for (send, _), x in zip(items, held)]


def along(axis, by):
    return lambda x: shift(x, axis, by)


def both_ways(axis, a, b):
    a, b = hold(a, b)
    return hold(shift(a, axis, 1), shift(b, axis, -1))


def over(*axes):
    return lambda x: flip(x, *axes)


def lay(parts, axis, q):
    shape = list(parts[0].shape)
    shape[axis] *= 4
    out = jnp.zeros(shape, parts[0].dtype)
    for d, part in enumerate(parts):
        out = put(out, part, q ^ d, axis)
    return out


def lay_ring(x, up, down, far, me):
    out = jnp.zeros((4 * x.shape[0], x.shape[1]), x.dtype)
    for k, part in ((0, x), (3, up), (1, down), (2, far)):
        out = put(out, part, (me + k) % 4, 0)
    return out


def ring_blocks(p, me):
    n = p.shape[0] // 4
    return [blk(p, (me + k) % 4, n, 0) for k in range(4)]


def x_join(g, gl, gh, gb, xl):
    first = xl == 0
    top = jnp.concatenate([jnp.where(first, g, gl), jnp.where(first, gh, gb)], 1)
    low = jnp.concatenate([jnp.where(first, gl, g), jnp.where(first, gb, gh)], 1)
    return jnp.concatenate([top, low], 0)


def pick(x, i):
    return lax.dynamic_index_in_dim(x, i, 0, keepdims=False)


def cat(*xs, axis=0):
    return jnp.concatenate(xs, axis)


def local(layer_input, out_grad, pre_act, w_in, w_out):
    z, xl, y, xh, c = (lax.axis_index(a) for a in ("z", "xl", "y", "xh", "c"))
    q = xh * 2 + c
    t_own, d_own = layer_input.shape
    f_dev = w_out.shape[0] // 4
    core, cross = over("c"), over("xh")
    f32 = lambda x: x.astype(F32)
    up, down = along("z", 1), along("z", -1)

    gl, gh, gb = over("xl")(out_grad), cross(out_grad), over("xl", "xh")(out_grad)
    wo4 = w_out.reshape(2, 2, f_dev, d_own)
    wo_here, wo_there = pick(wo4, xh), pick(wo4, 1 - xh)
    pa_here, pa_there = blk(pre_act, xh, 2 * f_dev, 1), blk(pre_act, 1 - xh, 2 * f_dev, 1)
    wo0, wo1 = pick(wo_here, c), core(pick(wo_here, 1 - c))
    wo_mine, wo_pass = pick(wo_there, c), pick(wo_there, 1 - c)
    pa0, pa1 = blk(pa_here, c, f_dev, 1), core(blk(pa_here, 1 - c, f_dev, 1))
    g0 = x_join(out_grad, gl, gh, gb, xl)
    h = g0.shape[0] // 2

    g0, pa_there, wo_mine, wo_pass, pa0 = hold(g0, pa_there, wo_mine, wo_pass, pa0)
    g3, g1, pa_got, wo3 = hold(up(g0), down(g0), cross(pa_there), cross(wo_pass))
    op_a, op_b, wo_mine, wo3 = hold(g3[:h], g1[h:], wo_mine, wo3)
    g2a, g2b, wo2 = up(op_a), down(op_b), cross(wo_mine)
    wo3 = core(wo3)
    pre_own = lay((pa0, pa1, blk(pa_got, c, f_dev, 1), core(blk(pa_got, 1 - c, f_dev, 1))), 0, q)
    pre = lax.all_gather(pre_own, "y", axis=0, tiled=True)
    slope = gelu_slope(f32(pre_own))
    g2a, g2b, wo2, wo3, slope, pre_own = hold(g2a, g2b, wo2, wo3, slope, pre_own)
    og = lay_ring(g0, g3, g1, cat(g2a, g2b), z)
    og_o = core(og)

    part = (dot_nt(og, cat(wo0, wo2, axis=1)) + dot_nt(og_o, cat(wo1, wo3, axis=1))).astype(BF)
    part, w_in, l_in, og, og_o = hold(part, w_in, layer_input, og, og_o)
    act_grad = lax.psum_scatter(part, "y", scatter_dimension=0, tiled=True)
    wi_here, wi_there = blk(w_in, xh, 2 * f_dev, 1), blk(w_in, 1 - xh, 2 * f_dev, 1)
    wi_got, ll = cross(wi_there), over("xl")(l_in)
    wi1 = core(blk(wi_here, 1 - c, f_dev, 1))
    first = xl == 0
    l_rows = cat(jnp.where(first, l_in, ll), jnp.where(first, ll, l_in))
    lh = cross(l_rows)
    act = gelu_act(f32(pre)).astype(BF)
    go = dot_tn(act, og).astype(BF)
    act_grad, wi_got, go = hold(act_grad, wi_got, go)
    h0 = (f32(act_grad) * slope).astype(BF)

    h0, li0, act = hold(h0, cat(l_rows, lh, axis=1), act)
    hidden = lax.all_gather(h0, "y", axis=0, tiled=True)
    li3, li1 = hold(up(li0), down(li0))
    op_a, op_b = hold(li3[:h], li1[h:])
    li2a, li2b = up(op_a), down(op_b)
    goo = dot_tn(act, og_o).astype(BF)
    wog_got = cross(cat(go[:, d_own:], goo[:, d_own:], axis=1))
    wi3 = core(blk(wi_got, 1 - c, f_dev, 1))
    va, vb = cat(blk(wi_here, c, f_dev, 1), blk(wi_got, c, f_dev, 1)), cat(wi1, wi3)
    li = lay_ring(li0, li3, li1, cat(li2a, li2b), z)
    hidden, va, vb, goo, wog_got, li = hold(hidden, va, vb, goo, wog_got, li)

    ig_o = core(dot_nt(hidden, vb).astype(BF))
    ig = (dot_nt(hidden, va) + f32(ig_o)).astype(BF)
    li_o = core(li)
    ig, hidden, goo, wog_got, li_o, og = hold(ig, hidden, goo, wog_got, li_o, og)
    ig = lax.psum_scatter(ig, "z", scatter_dimension=0, tiled=True)
    gi, gio = dot_tn(li, hidden).astype(BF), dot_tn(li_o, hidden).astype(BF)
    wig_got = cross(cat(gi[d_own:], gio[d_own:]))
    w1 = core(gio[:d_own])
    wog_rec = core(cat(goo[:, :d_own], wog_got[:, d_own:], axis=1))
    w_out_grad = lay((go[:, :d_own], wog_rec[:, :d_own], wog_got[:, :d_own], wog_rec[:, d_own:]), 0, q)
    b0 = jnp.sum(f32(hidden), axis=0)
    b1 = core(b0)
    b23 = cross(jnp.stack([b0, b1]))
    bias_in = lay((b0, b1, b23[0], b23[1]), 0, q)
    bias_out = jnp.sum(f32(og[:, :d_own]), axis=0)
    w3 = core(wig_got[d_own:])
    w_in_grad = lay((gi[:d_own], w1, wig_got[:d_own], w3), 1, q)
    ig, w_out_grad, bias_in, bias_out, wig_got = hold(ig, w_out_grad, bias_in, bias_out, wig_got)

    near, other = blk(ig, xl, t_own, 0), blk(ig, 1 - xl, t_own, 0)
    op_a, op_b, op_c = hold(other[:, :d_own], near[:, d_own:], other[:, d_own:])
    il, ih, ib = hold(over("xl")(op_a), cross(op_b), over("xl", "xh")(op_c))
    input_grad = (f32(near[:, :d_own]) + f32(il) + f32(ih) + f32(ib)).astype(BF)
    return input_grad, w_in_grad, w_out_grad, bias_in, bias_out


def solution(mesh):
    fine = Mesh(mesh.devices.reshape(tuple(SIZES.values())), tuple(SIZES))
    row, col = ("z", "xl"), ("y", "xh", "c")
    in_specs = (P(row, col), P(row, col), P(col, row), P(col, row), P(row, col))
    out_specs = (P(row, col), P(col, row), P(row, col), P(row), P(col))
    return jax.shard_map(local, mesh=fine, in_specs=in_specs, out_specs=out_specs, check_vma=False)
```

```python
import jax
import jax.numpy as jnp
from jax import lax
from jax.sharding import Mesh, PartitionSpec as P

SIZES = {"z": 4, "xl": 2, "y": 4, "xh": 2, "c": 2}
BF, F32 = jnp.bfloat16, jnp.float32


def gelu_act(v):
    return v * (0.5 * (1.0 + lax.erf(v * 0.7071067811865476)))


def gelu_slope(v):
    normal_cdf = 0.5 * (1.0 + lax.erf(v * 0.7071067811865476))
    normal_pdf = jnp.exp(-0.5 * v * v) * 0.3989422804014327
    return normal_cdf + v * normal_pdf


def shift(x, axis, by):
    n = SIZES[axis]
    return lax.ppermute(x, axis, [(i, (i + by) % n) for i in range(n)])


def flip(x, *axes):
    n = 2 ** len(axes)
    return lax.ppermute(x, axes if len(axes) > 1 else axes[0], [(i, n - 1 - i) for i in range(n)])


def dot_nt(a, b):
    return lax.dot_general(a, b, (((1,), (1,)), ((), ())), preferred_element_type=F32)


def dot_tn(a, b):
    return lax.dot_general(a, b, (((0,), (0,)), ((), ())), preferred_element_type=F32)


def blk(x, i, size, axis):
    return lax.dynamic_slice_in_dim(x, i * size, size, axis)


def put(buf, x, i, axis):
    return lax.dynamic_update_slice_in_dim(buf, x, i * x.shape[axis], axis)


def hold(*xs):
    return lax.optimization_barrier(xs)


def phase(tokens, *items):
    held = hold(*(x for _, x in items), *tokens)
    return [send(x) for (send, _), x in zip(items, held)]


def along(axis, by):
    return lambda x: shift(x, axis, by)


def both_ways(axis, a, b):
    a, b = hold(a, b)
    return hold(shift(a, axis, 1), shift(b, axis, -1))


def over(*axes):
    return lambda x: flip(x, *axes)


def lay(parts, axis, q):
    shape = list(parts[0].shape)
    shape[axis] *= 4
    out = jnp.zeros(shape, parts[0].dtype)
    for d, part in enumerate(parts):
        out = put(out, part, q ^ d, axis)
    return out


def lay_ring(x, up, down, far, me):
    out = jnp.zeros((4 * x.shape[0], x.shape[1]), x.dtype)
    for k, part in ((0, x), (3, up), (1, down), (2, far)):
        out = put(out, part, (me + k) % 4, 0)
    return out


def ring_blocks(p, me):
    n = p.shape[0] // 4
    return [blk(p, (me + k) % 4, n, 0) for k in range(4)]


def x_join(g, gl, gh, gb, xl):
    first = xl == 0
    top = jnp.concatenate([jnp.where(first, g, gl), jnp.where(first, gh, gb)], 1)
    low = jnp.concatenate([jnp.where(first, gl, g), jnp.where(first, gb, gh)], 1)
    return jnp.concatenate([top, low], 0)


def pick(x, i):
    return lax.dynamic_index_in_dim(x, i, 0, keepdims=False)


def cat(*xs, axis=0):
    return jnp.concatenate(xs, axis)


def local(layer_input, out_grad, pre_act, w_in, w_out):
    z, xl, y, xh, c = (lax.axis_index(a) for a in ("z", "xl", "y", "xh", "c"))
    q = xh * 2 + c
    t_own, d_own = layer_input.shape
    f_dev = w_out.shape[0] // 4
    core, cross = over("c"), over("xh")
    f32 = lambda x: x.astype(F32)
    up, down = along("z", 1), along("z", -1)

    gl, gh, gb = over("xl")(out_grad), cross(out_grad), over("xl", "xh")(out_grad)
    wo4 = w_out.reshape(2, 2, f_dev, d_own)
    wo_here, wo_there = pick(wo4, xh), pick(wo4, 1 - xh)
    pa_here, pa_there = blk(pre_act, xh, 2 * f_dev, 1), blk(pre_act, 1 - xh, 2 * f_dev, 1)
    wo0, wo1 = pick(wo_here, c), core(pick(wo_here, 1 - c))
    wo_mine, wo_pass = pick(wo_there, c), pick(wo_there, 1 - c)
    pa0, pa1 = blk(pa_here, c, f_dev, 1), core(blk(pa_here, 1 - c, f_dev, 1))
    g0 = x_join(out_grad, gl, gh, gb, xl)
    h = g0.shape[0] // 2

    g0, pa_there, wo_mine, wo_pass, pa0 = hold(g0, pa_there, wo_mine, wo_pass, pa0)
    g3, g1, pa_got, wo3 = hold(up(g0), down(g0), cross(pa_there), cross(wo_pass))
    op_a, op_b, wo_mine, wo3 = hold(g3[:h], g1[h:], wo_mine, wo3)
    g2a, g2b, wo2 = up(op_a), down(op_b), cross(wo_mine)
    wo3 = core(wo3)
    pre_own = lay((pa0, pa1, blk(pa_got, c, f_dev, 1), core(blk(pa_got, 1 - c, f_dev, 1))), 0, q)
    pre_up, pre_dn = along("y", 1)(pre_own), along("y", -1)(pre_own)
    slope = gelu_slope(f32(pre_own))
    g2a, g2b, wo2, wo3, slope = hold(g2a, g2b, wo2, wo3, slope)
    og = lay_ring(g0, g3, g1, cat(g2a, g2b), z)
    og_o = core(og)

    part = (dot_nt(og, cat(wo0, wo2, axis=1)) + dot_nt(og_o, cat(wo1, wo3, axis=1))).astype(BF)
    part, w_in, l_in, og, og_o, pre_up, pre_dn = hold(part, w_in, layer_input, og, og_o, pre_up, pre_dn)
    act_grad = lax.psum_scatter(part, "y", scatter_dimension=0, tiled=True)
    wi_here, wi_there = blk(w_in, xh, 2 * f_dev, 1), blk(w_in, 1 - xh, 2 * f_dev, 1)
    wi_got, ll = cross(wi_there), over("xl")(l_in)
    wi1 = core(blk(wi_here, 1 - c, f_dev, 1))
    first = xl == 0
    l_rows = cat(jnp.where(first, l_in, ll), jnp.where(first, ll, l_in))
    lh = cross(l_rows)
    hp = pre_own.shape[0] // 2
    pre_fa, pre_fb = hold(along("y", 1)(pre_up[:hp]), along("y", -1)(pre_dn[hp:]))
    pre = lay_ring(pre_own, pre_up, pre_dn, cat(pre_fa, pre_fb), y)
    act = gelu_act(f32(pre)).astype(BF)
    go = dot_tn(act, og).astype(BF)
    act_grad, wi_got, go = hold(act_grad, wi_got, go)
    h0 = (f32(act_grad) * slope).astype(BF)

    h0, li0, act = hold(h0, cat(l_rows, lh, axis=1), act)
    hidden = lax.all_gather(h0, "y", axis=0, tiled=True)
    li3, li1 = hold(up(li0), down(li0))
    op_a, op_b = hold(li3[:h], li1[h:])
    li2a, li2b = up(op_a), down(op_b)
    goo = dot_tn(act, og_o).astype(BF)
    wog_got = cross(cat(go[:, d_own:], goo[:, d_own:], axis=1))
    wi3 = core(blk(wi_got, 1 - c, f_dev, 1))
    va, vb = cat(blk(wi_here, c, f_dev, 1), blk(wi_got, c, f_dev, 1)), cat(wi1, wi3)
    li = lay_ring(li0, li3, li1, cat(li2a, li2b), z)
    hidden, va, vb, goo, wog_got, li = hold(hidden, va, vb, goo, wog_got, li)

    ig_o = core(dot_nt(hidden, vb).astype(BF))
    b0 = jnp.sum(f32(hidden), axis=0)
    b1 = core(b0)
    b23 = cross(jnp.stack([b0, b1]))
    ig = (dot_nt(hidden, va) + f32(ig_o)).astype(BF)
    ig, hidden, goo, wog_got, li, og, b23 = hold(ig, hidden, goo, wog_got, li, og, b23)
    ig = lax.psum_scatter(ig, "z", scatter_dimension=0, tiled=True)
    li_o = core(li)
    gi, gio = dot_tn(li, hidden).astype(BF), dot_tn(li_o, hidden).astype(BF)
    wig_far = cat(gi[d_own:], gio[d_own:])
    wig_got = cross(wig_far)
    wog_rec = core(cat(goo[:, :d_own], wog_got[:, d_own:], axis=1))
    w_out_grad = lay((go[:, :d_own], wog_rec[:, :d_own], wog_got[:, :d_own], wog_rec[:, d_own:]), 0, q)
    bias_in = lay((b0, b1, b23[0], b23[1]), 0, q)
    bias_out = jnp.sum(f32(og[:, :d_own]), axis=0)
    w1 = core(gio[:d_own])
    ig, w_out_grad, bias_in, bias_out, w1, wig_far = hold(ig, w_out_grad, bias_in, bias_out, w1, wig_far)

    near, other = blk(ig, xl, t_own, 0), blk(ig, 1 - xl, t_own, 0)
    op_a, op_b, op_c, w0, w1 = hold(other[:, :d_own], near[:, d_own:], other[:, d_own:], gi[:d_own], w1)
    il, ih, ib, wig_got = hold(over("xl")(op_a), cross(op_b), over("xl", "xh")(op_c), wig_got)
    w3 = core(wig_got[d_own:])
    w_in_grad = lay((w0, w1, wig_got[:d_own], w3), 1, q)
    input_grad = (f32(near[:, :d_own]) + f32(il) + f32(ih) + f32(ib)).astype(BF)
    return input_grad, w_in_grad, w_out_grad, bias_in, bias_out


def solution(mesh):
    fine = Mesh(mesh.devices.reshape(tuple(SIZES.values())), tuple(SIZES))
    row, col = ("z", "xl"), ("y", "xh", "c")
    in_specs = (P(row, col), P(row, col), P(col, row), P(col, row), P(row, col))
    out_specs = (P(row, col), P(col, row), P(row, col), P(row), P(col))
    return jax.shard_map(local, mesh=fine, in_specs=in_specs, out_specs=out_specs, check_vma=False)
```

```python
import jax
import jax.numpy as jnp
from jax import lax
from jax.sharding import Mesh, PartitionSpec as P

SIZES = {"z": 4, "xl": 2, "y": 4, "xh": 2, "c": 2}
BF, F32 = jnp.bfloat16, jnp.float32


def gelu_act(v):
    return v * (0.5 * (1.0 + lax.erf(v * 0.7071067811865476)))


def gelu_slope(v):
    normal_cdf = 0.5 * (1.0 + lax.erf(v * 0.7071067811865476))
    normal_pdf = jnp.exp(-0.5 * v * v) * 0.3989422804014327
    return normal_cdf + v * normal_pdf


def shift(x, axis, by):
    n = SIZES[axis]
    return lax.ppermute(x, axis, [(i, (i + by) % n) for i in range(n)])


def flip(x, *axes):
    n = 2 ** len(axes)
    return lax.ppermute(x, axes if len(axes) > 1 else axes[0], [(i, n - 1 - i) for i in range(n)])


def dot_nt(a, b):
    return lax.dot_general(a, b, (((1,), (1,)), ((), ())), preferred_element_type=F32)


def dot_tn(a, b):
    return lax.dot_general(a, b, (((0,), (0,)), ((), ())), preferred_element_type=F32)


def blk(x, i, size, axis):
    return lax.dynamic_slice_in_dim(x, i * size, size, axis)


def put(buf, x, i, axis):
    return lax.dynamic_update_slice_in_dim(buf, x, i * x.shape[axis], axis)


def hold(*xs):
    return lax.optimization_barrier(xs)


def phase(tokens, *items):
    held = hold(*(x for _, x in items), *tokens)
    return [send(x) for (send, _), x in zip(items, held)]


def along(axis, by):
    return lambda x: shift(x, axis, by)


def both_ways(axis, a, b):
    a, b = hold(a, b)
    return hold(shift(a, axis, 1), shift(b, axis, -1))


def over(*axes):
    return lambda x: flip(x, *axes)


def lay(parts, axis, q):
    shape = list(parts[0].shape)
    shape[axis] *= 4
    out = jnp.zeros(shape, parts[0].dtype)
    for d, part in enumerate(parts):
        out = put(out, part, q ^ d, axis)
    return out


def lay_ring(x, up, down, far, me):
    out = jnp.zeros((4 * x.shape[0], x.shape[1]), x.dtype)
    for k, part in ((0, x), (3, up), (1, down), (2, far)):
        out = put(out, part, (me + k) % 4, 0)
    return out


def ring_blocks(p, me):
    n = p.shape[0] // 4
    return [blk(p, (me + k) % 4, n, 0) for k in range(4)]


def x_join(g, gl, gh, gb, xl):
    first = xl == 0
    top = jnp.concatenate([jnp.where(first, g, gl), jnp.where(first, gh, gb)], 1)
    low = jnp.concatenate([jnp.where(first, gl, g), jnp.where(first, gb, gh)], 1)
    return jnp.concatenate([top, low], 0)


def pick(x, i):
    return lax.dynamic_index_in_dim(x, i, 0, keepdims=False)


def cat(*xs, axis=0):
    return jnp.concatenate(xs, axis)


def local(layer_input, out_grad, pre_act, w_in, w_out):
    z, xl, y, xh, c = (lax.axis_index(a) for a in ("z", "xl", "y", "xh", "c"))
    q = xh * 2 + c
    t_own, d_own = layer_input.shape
    f_dev = w_out.shape[0] // 4
    core, cross = over("c"), over("xh")
    f32 = lambda x: x.astype(F32)
    up, down = along("z", 1), along("z", -1)

    gl, gh, gb = over("xl")(out_grad), cross(out_grad), over("xl", "xh")(out_grad)
    wo4 = w_out.reshape(2, 2, f_dev, d_own)
    wo_here, wo_there = pick(wo4, xh), pick(wo4, 1 - xh)
    pa_here, pa_there = blk(pre_act, xh, 2 * f_dev, 1), blk(pre_act, 1 - xh, 2 * f_dev, 1)
    wo0, wo1 = pick(wo_here, c), core(pick(wo_here, 1 - c))
    wo_mine, wo_pass = pick(wo_there, c), pick(wo_there, 1 - c)
    pa0, pa1 = blk(pa_here, c, f_dev, 1), core(blk(pa_here, 1 - c, f_dev, 1))
    g0 = x_join(out_grad, gl, gh, gb, xl)
    h = g0.shape[0] // 2

    g0, pa_there, wo_mine, wo_pass, pa0, wo1 = hold(g0, pa_there, wo_mine, wo_pass, pa0, wo1)
    g3, g1, pa_got = up(g0), down(g0), cross(pa_there)
    wo_pass, pa_got = hold(wo_pass, pa_got)
    wo3 = cross(wo_pass)
    pre_own = lay((pa0, pa1, blk(pa_got, c, f_dev, 1), core(blk(pa_got, 1 - c, f_dev, 1))), 0, q)
    pre_up, pre_dn = along("y", 1)(pre_own), along("y", -1)(pre_own)
    slope = gelu_slope(f32(pre_own))
    g3, g1 = hold(g3, g1)
    op_a, op_b = hold(g3[:h], g1[h:])
    g2a, g2b = up(op_a), down(op_b)
    wo_mine, wo3 = hold(wo_mine, wo3)
    wo2 = cross(wo_mine)
    g2a, g2b, wo2, wo3, slope, pre_up, pre_dn = hold(g2a, g2b, wo2, wo3, slope, pre_up, pre_dn)
    og = lay_ring(g0, g3, g1, cat(g2a, g2b), z)
    hp = pre_own.shape[0] // 2
    og, pre_a, pre_b, l_in = hold(og, pre_up[:hp], pre_dn[hp:], layer_input)
    og_o, wo3 = core(og), core(wo3)
    pre_fa, pre_fb, ll = along("y", 1)(pre_a), along("y", -1)(pre_b), over("xl")(l_in)

    part = (dot_nt(og, cat(wo0, wo2, axis=1)) + dot_nt(og_o, cat(wo1, wo3, axis=1))).astype(BF)
    part, w_in, og, og_o, pre_fa, pre_fb, ll = hold(part, w_in, og, og_o, pre_fa, pre_fb, ll)
    act_grad = lax.psum_scatter(part, "y", scatter_dimension=0, tiled=True)
    wi_here, wi_there = blk(w_in, xh, 2 * f_dev, 1), blk(w_in, 1 - xh, 2 * f_dev, 1)
    first = xl == 0
    l_rows = cat(jnp.where(first, l_in, ll), jnp.where(first, ll, l_in))
    lh = cross(l_rows)
    wi_there, lh = hold(wi_there, lh)
    wi_got = cross(wi_there)
    wi1 = core(blk(wi_here, 1 - c, f_dev, 1))
    pre = lay_ring(pre_own, pre_up, pre_dn, cat(pre_fa, pre_fb), y)
    act = gelu_act(f32(pre)).astype(BF)
    go = dot_tn(act, og).astype(BF)
    act_grad, lh, go, wi_got = hold(act_grad, lh, go, wi_got)
    h0 = (f32(act_grad) * slope).astype(BF)

    h0, li0, act = hold(h0, cat(l_rows, lh, axis=1), act)
    hidden = lax.all_gather(h0, "y", axis=0, tiled=True)
    li3, li1 = hold(up(li0), down(li0))
    op_a, op_b = hold(li3[:h], li1[h:])
    li2a, li2b = up(op_a), down(op_b)
    goo = dot_tn(act, og_o).astype(BF)
    wog_got = cross(cat(go[:, d_own:], goo[:, d_own:], axis=1))
    wi3 = core(blk(wi_got, 1 - c, f_dev, 1))
    va, vb = cat(blk(wi_here, c, f_dev, 1), blk(wi_got, c, f_dev, 1)), cat(wi1, wi3)
    li = lay_ring(li0, li3, li1, cat(li2a, li2b), z)
    li_o = core(li)
    hidden, va, vb, goo, wog_got, li = hold(hidden, va, vb, goo, wog_got, li)

    n = hidden.shape[0] // 2
    ig_a, li_o = hold(dot_nt(hidden[:n], vb).astype(BF), li_o)
    ig_a, ig_b = core(ig_a), core(dot_nt(hidden[n:], vb).astype(BF))
    b0 = jnp.sum(f32(hidden), axis=0)
    b1 = core(b0)
    b23 = cross(jnp.stack([b0, b1]))
    ig = (dot_nt(hidden, va) + f32(cat(ig_a, ig_b))).astype(BF)
    ig, hidden, goo, wog_got, li, og, b23 = hold(ig, hidden, goo, wog_got, li, og, b23)
    ig = lax.psum_scatter(ig, "z", scatter_dimension=0, tiled=True)
    wig_far = cat(dot_tn(li[:, d_own:], hidden).astype(BF), dot_tn(li_o[:, d_own:], hidden).astype(BF))
    wig_got = cross(wig_far)
    h_near = hold(hidden, wig_far)[0]
    w0, w1 = dot_tn(li[:, :d_own], h_near).astype(BF), core(dot_tn(li_o[:, :d_own], h_near).astype(BF))
    wog_rec = core(cat(goo[:, :d_own], wog_got[:, d_own:], axis=1))
    w_out_grad = lay((go[:, :d_own], wog_rec[:, :d_own], wog_got[:, :d_own], wog_rec[:, d_own:]), 0, q)
    bias_in = lay((b0, b1, b23[0], b23[1]), 0, q)
    bias_out = jnp.sum(f32(og[:, :d_own]), axis=0)
    ig, w_out_grad, bias_in, bias_out, w1, wig_far = hold(ig, w_out_grad, bias_in, bias_out, w1, wig_far)

    near, other = blk(ig, xl, t_own, 0), blk(ig, 1 - xl, t_own, 0)
    op_a, op_b, op_c, w0, w1 = hold(other[:, :d_own], near[:, d_own:], other[:, d_own:], w0, w1)
    il, ih, ib, wig_got = hold(over("xl")(op_a), cross(op_b), over("xl", "xh")(op_c), wig_got)
    w3 = core(wig_got[d_own:])
    w_in_grad = lay((w0, w1, wig_got[:d_own], w3), 1, q)
    input_grad = (f32(near[:, :d_own]) + f32(il) + f32(ih) + f32(ib)).astype(BF)
    return input_grad, w_in_grad, w_out_grad, bias_in, bias_out


def solution(mesh):
    fine = Mesh(mesh.devices.reshape(tuple(SIZES.values())), tuple(SIZES))
    row, col = ("z", "xl"), ("y", "xh", "c")
    in_specs = (P(row, col), P(row, col), P(col, row), P(col, row), P(row, col))
    out_specs = (P(row, col), P(col, row), P(row, col), P(row), P(col))
    return jax.shard_map(local, mesh=fine, in_specs=in_specs, out_specs=out_specs, check_vma=False)
```

```python
import jax
import jax.numpy as jnp
from jax import lax
from jax.sharding import Mesh, PartitionSpec as P

SIZES = {"z": 4, "xl": 2, "y": 4, "xh": 2, "c": 2}
BF, F32 = jnp.bfloat16, jnp.float32


def gelu_act(v):
    return v * (0.5 * (1.0 + lax.erf(v * 0.7071067811865476)))


def gelu_slope(v):
    normal_cdf = 0.5 * (1.0 + lax.erf(v * 0.7071067811865476))
    normal_pdf = jnp.exp(-0.5 * v * v) * 0.3989422804014327
    return normal_cdf + v * normal_pdf


def shift(x, axis, by):
    n = SIZES[axis]
    return lax.ppermute(x, axis, [(i, (i + by) % n) for i in range(n)])


def flip(x, *axes):
    n = 2 ** len(axes)
    return lax.ppermute(x, axes if len(axes) > 1 else axes[0], [(i, n - 1 - i) for i in range(n)])


def dot_nt(a, b):
    return lax.dot_general(a, b, (((1,), (1,)), ((), ())), preferred_element_type=F32)


def dot_tn(a, b):
    return lax.dot_general(a, b, (((0,), (0,)), ((), ())), preferred_element_type=F32)


def blk(x, i, size, axis):
    return lax.dynamic_slice_in_dim(x, i * size, size, axis)


def put(buf, x, i, axis):
    return lax.dynamic_update_slice_in_dim(buf, x, i * x.shape[axis], axis)


def hold(*xs):
    return lax.optimization_barrier(xs)


def phase(tokens, *items):
    held = hold(*(x for _, x in items), *tokens)
    return [send(x) for (send, _), x in zip(items, held)]


def along(axis, by):
    return lambda x: shift(x, axis, by)


def both_ways(axis, a, b):
    a, b = hold(a, b)
    return hold(shift(a, axis, 1), shift(b, axis, -1))


def over(*axes):
    return lambda x: flip(x, *axes)


def lay(parts, axis, q):
    shape = list(parts[0].shape)
    shape[axis] *= 4
    out = jnp.zeros(shape, parts[0].dtype)
    for d, part in enumerate(parts):
        out = put(out, part, q ^ d, axis)
    return out


def lay_ring(x, up, down, far, me):
    out = jnp.zeros((4 * x.shape[0], x.shape[1]), x.dtype)
    for k, part in ((0, x), (3, up), (1, down), (2, far)):
        out = put(out, part, (me + k) % 4, 0)
    return out


def ring_blocks(p, me):
    n = p.shape[0] // 4
    return [blk(p, (me + k) % 4, n, 0) for k in range(4)]


def x_join(g, gl, gh, gb, xl):
    first = xl == 0
    top = jnp.concatenate([jnp.where(first, g, gl), jnp.where(first, gh, gb)], 1)
    low = jnp.concatenate([jnp.where(first, gl, g), jnp.where(first, gb, gh)], 1)
    return jnp.concatenate([top, low], 0)


def pick(x, i):
    return lax.dynamic_index_in_dim(x, i, 0, keepdims=False)


def cat(*xs, axis=0):
    return jnp.concatenate(xs, axis)


def local(layer_input, out_grad, pre_act, w_in, w_out):
    z, xl, y, xh, c = (lax.axis_index(a) for a in ("z", "xl", "y", "xh", "c"))
    q = xh * 2 + c
    t_own, d_own = layer_input.shape
    f_dev = w_out.shape[0] // 4
    core, cross = over("c"), over("xh")
    f32 = lambda x: x.astype(F32)
    up, down = along("z", 1), along("z", -1)

    gl, gh, gb = over("xl")(out_grad), cross(out_grad), over("xl", "xh")(out_grad)
    wo4 = w_out.reshape(2, 2, f_dev, d_own)
    wo_here, wo_there = pick(wo4, xh), pick(wo4, 1 - xh)
    pa_here, pa_there = blk(pre_act, xh, 2 * f_dev, 1), blk(pre_act, 1 - xh, 2 * f_dev, 1)
    wo0, wo1 = pick(wo_here, c), core(pick(wo_here, 1 - c))
    wo_mine, wo_pass = pick(wo_there, c), pick(wo_there, 1 - c)
    pa0, pa1 = blk(pa_here, c, f_dev, 1), core(blk(pa_here, 1 - c, f_dev, 1))
    g0 = x_join(out_grad, gl, gh, gb, xl)
    h = g0.shape[0] // 2

    g0, pa_there, wo_mine, wo_pass, pa0, wo1 = hold(g0, pa_there, wo_mine, wo_pass, pa0, wo1)
    g3, g1, pa_got = up(g0), down(g0), cross(pa_there)
    wo_pass, pa_got = hold(wo_pass, pa_got)
    wo3 = cross(wo_pass)
    pre_own = lay((pa0, pa1, blk(pa_got, c, f_dev, 1), core(blk(pa_got, 1 - c, f_dev, 1))), 0, q)
    pre_up, pre_dn = along("y", 1)(pre_own), along("y", -1)(pre_own)
    slope = gelu_slope(f32(pre_own))
    g3, g1 = hold(g3, g1)
    op_a, op_b = hold(g3[:h], g1[h:])
    g2a, g2b = up(op_a), down(op_b)
    wo_mine, wo3 = hold(wo_mine, wo3)
    wo2 = cross(wo_mine)
    g2a, g2b, wo2, wo3, slope, pre_up, pre_dn = hold(g2a, g2b, wo2, wo3, slope, pre_up, pre_dn)
    og = lay_ring(g0, g3, g1, cat(g2a, g2b), z)
    hp = pre_own.shape[0] // 2
    og, pre_a, pre_b, l_in = hold(og, pre_up[:hp], pre_dn[hp:], layer_input)
    og_o, wo3 = core(og), core(wo3)
    pre_fa, pre_fb, ll = along("y", 1)(pre_a), along("y", -1)(pre_b), over("xl")(l_in)

    part = (dot_nt(og, cat(wo0, wo2, axis=1)) + dot_nt(og_o, cat(wo1, wo3, axis=1))).astype(BF)
    part, w_in, og, og_o, pre_fa, pre_fb, ll = hold(part, w_in, og, og_o, pre_fa, pre_fb, ll)
    act_grad = lax.psum_scatter(part, "y", scatter_dimension=0, tiled=True)
    wi_here, wi_there = blk(w_in, xh, 2 * f_dev, 1), blk(w_in, 1 - xh, 2 * f_dev, 1)
    first = xl == 0
    l_rows = cat(jnp.where(first, l_in, ll), jnp.where(first, ll, l_in))
    lh = cross(l_rows)
    wi_there, lh = hold(wi_there, lh)
    wi_got = cross(wi_there)
    wi1 = core(blk(wi_here, 1 - c, f_dev, 1))
    pre = lay_ring(pre_own, pre_up, pre_dn, cat(pre_fa, pre_fb), y)
    act = gelu_act(f32(pre)).astype(BF)
    go = dot_tn(act, og).astype(BF)
    goo = dot_tn(act, og_o).astype(BF)
    wog_far = cat(go[:, d_own:], goo[:, d_own:], axis=1)
    act_grad, lh, wog_far, wi_got = hold(act_grad, lh, wog_far, wi_got)
    h0 = (f32(act_grad) * slope).astype(BF)

    h0, li0, wog_far = hold(h0, cat(l_rows, lh, axis=1), wog_far)
    wog_got = cross(wog_far)
    hidden = lax.all_gather(h0, "y", axis=0, tiled=True)
    li3, li1 = hold(up(li0), down(li0))
    op_a, op_b = hold(li3[:h], li1[h:])
    li2a, li2b, wog_got = hold(up(op_a), down(op_b), wog_got)
    wi3 = core(blk(wi_got, 1 - c, f_dev, 1))
    va, vb = cat(blk(wi_here, c, f_dev, 1), blk(wi_got, c, f_dev, 1)), cat(wi1, wi3)
    li = lay_ring(li0, li3, li1, cat(li2a, li2b), z)
    li_o = core(li)
    hidden, va, vb, goo, wog_got, li, li_o = hold(hidden, va, vb, goo, wog_got, li, li_o)

    n = hidden.shape[0] // 2
    ig_a, ig_b = core(dot_nt(hidden[:n], vb).astype(BF)), core(dot_nt(hidden[n:], vb).astype(BF))
    ig = (dot_nt(hidden, va) + f32(cat(ig_a, ig_b))).astype(BF)
    ig, hidden, goo, wog_got, li, og = hold(ig, hidden, goo, wog_got, li, og)
    ig = lax.psum_scatter(ig, "z", scatter_dimension=0, tiled=True)
    wig_far = cat(dot_tn(li[:, d_own:], hidden).astype(BF), dot_tn(li_o[:, d_own:], hidden).astype(BF))
    b0 = jnp.sum(f32(hidden), axis=0)
    b1 = core(b0)
    b23 = cross(jnp.stack([b0, b1]))
    wig_far, b23 = hold(wig_far, b23)
    wig_got = cross(wig_far)
    h_near = hold(hidden, wig_far)[0]
    w0, w1 = dot_tn(li[:, :d_own], h_near).astype(BF), core(dot_tn(li_o[:, :d_own], h_near).astype(BF))
    wog_rec = core(cat(goo[:, :d_own], wog_got[:, d_own:], axis=1))
    w_out_grad = lay((go[:, :d_own], wog_rec[:, :d_own], wog_got[:, :d_own], wog_rec[:, d_own:]), 0, q)
    bias_in = lay((b0, b1, b23[0], b23[1]), 0, q)
    bias_out = jnp.sum(f32(og[:, :d_own]), axis=0)
    ig, w_out_grad, bias_in, bias_out, w1, wig_got = hold(ig, w_out_grad, bias_in, bias_out, w1, wig_got)

    near, other = blk(ig, xl, t_own, 0), blk(ig, 1 - xl, t_own, 0)
    op_a, op_b, op_c, w0, w1, wig_got = hold(other[:, :d_own], near[:, d_own:], other[:, d_own:], w0, w1, wig_got)
    il, ih, ib = hold(over("xl")(op_a), cross(op_b), over("xl", "xh")(op_c))
    w3 = core(wig_got[d_own:])
    w_in_grad = lay((w0, w1, wig_got[:d_own], w3), 1, q)
    input_grad = (f32(near[:, :d_own]) + f32(il) + f32(ih) + f32(ib)).astype(BF)
    return input_grad, w_in_grad, w_out_grad, bias_in, bias_out


def solution(mesh):
    fine = Mesh(mesh.devices.reshape(tuple(SIZES.values())), tuple(SIZES))
    row, col = ("z", "xl"), ("y", "xh", "c")
    in_specs = (P(row, col), P(row, col), P(col, row), P(col, row), P(row, col))
    out_specs = (P(row, col), P(col, row), P(row, col), P(row), P(col))
    return jax.shard_map(local, mesh=fine, in_specs=in_specs, out_specs=out_specs, check_vma=False)
```

```python
import jax
import jax.numpy as jnp
from jax import lax
from jax.sharding import Mesh, PartitionSpec as P

SIZES = {"z": 4, "xl": 2, "y": 4, "xh": 2, "c": 2}
BF, F32 = jnp.bfloat16, jnp.float32


def gelu_act(v):
    return v * (0.5 * (1.0 + lax.erf(v * 0.7071067811865476)))


def gelu_slope(v):
    normal_cdf = 0.5 * (1.0 + lax.erf(v * 0.7071067811865476))
    normal_pdf = jnp.exp(-0.5 * v * v) * 0.3989422804014327
    return normal_cdf + v * normal_pdf


def shift(x, axis, by):
    n = SIZES[axis]
    return lax.ppermute(x, axis, [(i, (i + by) % n) for i in range(n)])


def flip(x, *axes):
    n = 2 ** len(axes)
    return lax.ppermute(x, axes if len(axes) > 1 else axes[0], [(i, n - 1 - i) for i in range(n)])


def dot_nt(a, b):
    return lax.dot_general(a, b, (((1,), (1,)), ((), ())), preferred_element_type=F32)


def dot_tn(a, b):
    return lax.dot_general(a, b, (((0,), (0,)), ((), ())), preferred_element_type=F32)


def blk(x, i, size, axis):
    return lax.dynamic_slice_in_dim(x, i * size, size, axis)


def put(buf, x, i, axis):
    return lax.dynamic_update_slice_in_dim(buf, x, i * x.shape[axis], axis)


def hold(*xs):
    return lax.optimization_barrier(xs)


def phase(tokens, *items):
    held = hold(*(x for _, x in items), *tokens)
    return [send(x) for (send, _), x in zip(items, held)]


def along(axis, by):
    return lambda x: shift(x, axis, by)


def both_ways(axis, a, b):
    a, b = hold(a, b)
    return hold(shift(a, axis, 1), shift(b, axis, -1))


def over(*axes):
    return lambda x: flip(x, *axes)


def lay(parts, axis, q):
    shape = list(parts[0].shape)
    shape[axis] *= 4
    out = jnp.zeros(shape, parts[0].dtype)
    for d, part in enumerate(parts):
        out = put(out, part, q ^ d, axis)
    return out


def lay_ring(x, up, down, far, me):
    out = jnp.zeros((4 * x.shape[0], x.shape[1]), x.dtype)
    for k, part in ((0, x), (3, up), (1, down), (2, far)):
        out = put(out, part, (me + k) % 4, 0)
    return out


def ring_blocks(p, me):
    n = p.shape[0] // 4
    return [blk(p, (me + k) % 4, n, 0) for k in range(4)]


def x_join(g, gl, gh, gb, xl):
    first = xl == 0
    top = jnp.concatenate([jnp.where(first, g, gl), jnp.where(first, gh, gb)], 1)
    low = jnp.concatenate([jnp.where(first, gl, g), jnp.where(first, gb, gh)], 1)
    return jnp.concatenate([top, low], 0)


def pick(x, i):
    return lax.dynamic_index_in_dim(x, i, 0, keepdims=False)


def cat(*xs, axis=0):
    return jnp.concatenate(xs, axis)


def local(layer_input, out_grad, pre_act, w_in, w_out):
    z, xl, y, xh, c = (lax.axis_index(a) for a in ("z", "xl", "y", "xh", "c"))
    q = xh * 2 + c
    t_own, d_own = layer_input.shape
    f_dev = w_out.shape[0] // 4
    core, cross = over("c"), over("xh")
    f32 = lambda x: x.astype(F32)
    up, down = along("z", 1), along("z", -1)

    gl, gh, gb = over("xl")(out_grad), cross(out_grad), over("xl", "xh")(out_grad)
    wo4 = w_out.reshape(2, 2, f_dev, d_own)
    wo_here, wo_there = pick(wo4, xh), pick(wo4, 1 - xh)
    pa_here, pa_there = blk(pre_act, xh, 2 * f_dev, 1), blk(pre_act, 1 - xh, 2 * f_dev, 1)
    wo0, wo1 = pick(wo_here, c), core(pick(wo_here, 1 - c))
    wo_mine, wo_pass = pick(wo_there, c), pick(wo_there, 1 - c)
    pa0, pa1 = blk(pa_here, c, f_dev, 1), core(blk(pa_here, 1 - c, f_dev, 1))
    g0 = x_join(out_grad, gl, gh, gb, xl)
    h = g0.shape[0] // 2

    g0, pa_there, wo_mine, wo_pass, pa0, wo1 = hold(g0, pa_there, wo_mine, wo_pass, pa0, wo1)
    g3, g1, pa_got = up(g0), down(g0), cross(pa_there)
    wo_pass, pa_got = hold(wo_pass, pa_got)
    wo3 = cross(wo_pass)
    pre_own = lay((pa0, pa1, blk(pa_got, c, f_dev, 1), core(blk(pa_got, 1 - c, f_dev, 1))), 0, q)
    pre_up, pre_dn = along("y", 1)(pre_own), along("y", -1)(pre_own)
    slope = gelu_slope(f32(pre_own))
    g3, g1 = hold(g3, g1)
    op_a, op_b = hold(g3[:h], g1[h:])
    g2a, g2b = up(op_a), down(op_b)
    wo_mine, wo3 = hold(wo_mine, wo3)
    wo2 = cross(wo_mine)
    g2a, g2b, wo2, wo3, slope, pre_up, pre_dn = hold(g2a, g2b, wo2, wo3, slope, pre_up, pre_dn)
    og = lay_ring(g0, g3, g1, cat(g2a, g2b), z)
    hp = pre_own.shape[0] // 2
    og, pre_a, pre_b, l_in = hold(og, pre_up[:hp], pre_dn[hp:], layer_input)
    og_o, wo3 = core(og), core(wo3)
    pre_fa, pre_fb, ll = along("y", 1)(pre_a), along("y", -1)(pre_b), over("xl")(l_in)

    part = (dot_nt(og, cat(wo0, wo2, axis=1)) + dot_nt(og_o, cat(wo1, wo3, axis=1))).astype(BF)
    part, w_in, og, og_o, pre_fa, pre_fb, ll = hold(part, w_in, og, og_o, pre_fa, pre_fb, ll)
    act_grad = lax.psum_scatter(part, "y", scatter_dimension=0, tiled=True)
    wi_here, wi_there = blk(w_in, xh, 2 * f_dev, 1), blk(w_in, 1 - xh, 2 * f_dev, 1)
    first = xl == 0
    l_rows = cat(jnp.where(first, l_in, ll), jnp.where(first, ll, l_in))
    lh = cross(l_rows)
    wi_got = cross(wi_there)
    wi1 = core(blk(wi_here, 1 - c, f_dev, 1))
    pre = lay_ring(pre_own, pre_up, pre_dn, cat(pre_fa, pre_fb), y)
    act = gelu_act(f32(pre)).astype(BF)
    go = dot_tn(act, og).astype(BF)
    goo = dot_tn(act, og_o).astype(BF)
    wog_far = cat(go[:, d_own:], goo[:, d_own:], axis=1)
    act_grad, li0, wog_far, wi_got = hold(act_grad, cat(l_rows, lh, axis=1), wog_far, wi_got)
    h0 = (f32(act_grad) * slope).astype(BF)

    h0, li0, wog_far = hold(h0, li0, wog_far)
    wog_got = cross(wog_far)
    hidden = lax.all_gather(h0, "y", axis=0, tiled=True)
    li3, li1 = hold(up(li0), down(li0))
    op_a, op_b = hold(li3[:h], li1[h:])
    li2a, li2b, wog_got = hold(up(op_a), down(op_b), wog_got)
    wi3 = core(blk(wi_got, 1 - c, f_dev, 1))
    va, vb = cat(blk(wi_here, c, f_dev, 1), blk(wi_got, c, f_dev, 1)), cat(wi1, wi3)
    li = lay_ring(li0, li3, li1, cat(li2a, li2b), z)
    li_o = core(li)
    hidden, va, vb, goo, wog_got, li, li_o = hold(hidden, va, vb, goo, wog_got, li, li_o)

    n = hidden.shape[0] // 2
    ig_a, ig_b = core(dot_nt(hidden[:n], vb).astype(BF)), core(dot_nt(hidden[n:], vb).astype(BF))
    ig = (hold(dot_nt(hidden, va), hidden)[0] + f32(cat(ig_a, ig_b))).astype(BF)
    ig, hidden, goo, wog_got, li, og = hold(ig, hidden, goo, wog_got, li, og)
    ig = lax.psum_scatter(ig, "z", scatter_dimension=0, tiled=True)
    wig_far = cat(dot_tn(li[:, d_own:], hidden).astype(BF), dot_tn(li_o[:, d_own:], hidden).astype(BF))
    b0 = jnp.sum(f32(hidden), axis=0)
    b1 = core(b0)
    b23 = cross(jnp.stack([b0, b1]))
    wig_far, b23, go, goo, wog_got, og = hold(wig_far, b23, go, goo, wog_got, og)
    wig_got = cross(wig_far)
    h_near = hold(hidden, wig_far)[0]
    w0, w1 = dot_tn(li[:, :d_own], h_near).astype(BF), core(dot_tn(li_o[:, :d_own], h_near).astype(BF))
    wog_rec = core(cat(goo[:, :d_own], wog_got[:, d_own:], axis=1))
    w_out_grad = lay((go[:, :d_own], wog_rec[:, :d_own], wog_got[:, :d_own], wog_rec[:, d_own:]), 0, q)
    bias_in = lay((b0, b1, b23[0], b23[1]), 0, q)
    bias_out = jnp.sum(f32(og[:, :d_own]), axis=0)
    ig, w_out_grad, bias_in, bias_out, w1, wig_got = hold(ig, w_out_grad, bias_in, bias_out, w1, wig_got)

    near, other = blk(ig, xl, t_own, 0), blk(ig, 1 - xl, t_own, 0)
    op_a, op_b, op_c, w0, w1, wig_got = hold(other[:, :d_own], near[:, d_own:], other[:, d_own:], w0, w1, wig_got)
    il, ih, ib = hold(over("xl")(op_a), cross(op_b), over("xl", "xh")(op_c))
    w3 = core(wig_got[d_own:])
    w_in_grad = lay((w0, w1, wig_got[:d_own], w3), 1, q)
    input_grad = (f32(near[:, :d_own]) + f32(il) + f32(ih) + f32(ib)).astype(BF)
    return input_grad, w_in_grad, w_out_grad, bias_in, bias_out


def solution(mesh):
    fine = Mesh(mesh.devices.reshape(tuple(SIZES.values())), tuple(SIZES))
    row, col = ("z", "xl"), ("y", "xh", "c")
    in_specs = (P(row, col), P(row, col), P(col, row), P(col, row), P(row, col))
    out_specs = (P(row, col), P(col, row), P(row, col), P(row), P(col))
    return jax.shard_map(local, mesh=fine, in_specs=in_specs, out_specs=out_specs, check_vma=False)
```

```python
import jax
import jax.numpy as jnp
from jax import lax
from jax.sharding import Mesh, PartitionSpec as P

SIZES = {"z": 4, "xl": 2, "y": 4, "xh": 2, "c": 2}
BF, F32 = jnp.bfloat16, jnp.float32


def gelu_act(v):
    return v * (0.5 * (1.0 + lax.erf(v * 0.7071067811865476)))


def gelu_slope(v):
    normal_cdf = 0.5 * (1.0 + lax.erf(v * 0.7071067811865476))
    normal_pdf = jnp.exp(-0.5 * v * v) * 0.3989422804014327
    return normal_cdf + v * normal_pdf


def shift(x, axis, by):
    n = SIZES[axis]
    return lax.ppermute(x, axis, [(i, (i + by) % n) for i in range(n)])


def flip(x, *axes):
    n = 2 ** len(axes)
    return lax.ppermute(x, axes if len(axes) > 1 else axes[0], [(i, n - 1 - i) for i in range(n)])


def dot_nt(a, b):
    return lax.dot_general(a, b, (((1,), (1,)), ((), ())), preferred_element_type=F32)


def dot_tn(a, b):
    return lax.dot_general(a, b, (((0,), (0,)), ((), ())), preferred_element_type=F32)


def blk(x, i, size, axis):
    return lax.dynamic_slice_in_dim(x, i * size, size, axis)


def put(buf, x, i, axis):
    return lax.dynamic_update_slice_in_dim(buf, x, i * x.shape[axis], axis)


def hold(*xs):
    return lax.optimization_barrier(xs)


def phase(tokens, *items):
    held = hold(*(x for _, x in items), *tokens)
    return [send(x) for (send, _), x in zip(items, held)]


def along(axis, by):
    return lambda x: shift(x, axis, by)


def both_ways(axis, a, b):
    a, b = hold(a, b)
    return hold(shift(a, axis, 1), shift(b, axis, -1))


def over(*axes):
    return lambda x: flip(x, *axes)


def lay(parts, axis, q):
    shape = list(parts[0].shape)
    shape[axis] *= 4
    out = jnp.zeros(shape, parts[0].dtype)
    for d, part in enumerate(parts):
        out = put(out, part, q ^ d, axis)
    return out


def lay_ring(x, up, down, far, me):
    out = jnp.zeros((4 * x.shape[0], x.shape[1]), x.dtype)
    for k, part in ((0, x), (3, up), (1, down), (2, far)):
        out = put(out, part, (me + k) % 4, 0)
    return out


def ring_blocks(p, me):
    n = p.shape[0] // 4
    return [blk(p, (me + k) % 4, n, 0) for k in range(4)]


def x_join(g, gl, gh, gb, xl):
    first = xl == 0
    top = jnp.concatenate([jnp.where(first, g, gl), jnp.where(first, gh, gb)], 1)
    low = jnp.concatenate([jnp.where(first, gl, g), jnp.where(first, gb, gh)], 1)
    return jnp.concatenate([top, low], 0)


def pick(x, i):
    return lax.dynamic_index_in_dim(x, i, 0, keepdims=False)


def cat(*xs, axis=0):
    return jnp.concatenate(xs, axis)


def local(layer_input, out_grad, pre_act, w_in, w_out):
    z, xl, y, xh, c = (lax.axis_index(a) for a in ("z", "xl", "y", "xh", "c"))
    q = xh * 2 + c
    t_own, d_own = layer_input.shape
    f_dev = w_out.shape[0] // 4
    core, cross = over("c"), over("xh")
    f32 = lambda x: x.astype(F32)
    up, down = along("z", 1), along("z", -1)

    gl, gh, gb = over("xl")(out_grad), cross(out_grad), over("xl", "xh")(out_grad)
    wo4 = w_out.reshape(2, 2, f_dev, d_own)
    wo_here, wo_there = pick(wo4, xh), pick(wo4, 1 - xh)
    pa_here, pa_there = blk(pre_act, xh, 2 * f_dev, 1), blk(pre_act, 1 - xh, 2 * f_dev, 1)
    wo0, wo1 = pick(wo_here, c), core(pick(wo_here, 1 - c))
    wo_mine, wo_pass = pick(wo_there, c), pick(wo_there, 1 - c)
    pa0, pa1 = blk(pa_here, c, f_dev, 1), core(blk(pa_here, 1 - c, f_dev, 1))
    g0 = x_join(out_grad, gl, gh, gb, xl)
    h = g0.shape[0] // 2

    g0, pa_there, wo_mine, wo_pass, pa0, wo1 = hold(g0, pa_there, wo_mine, wo_pass, pa0, wo1)
    g3, g1, pa_got = up(g0), down(g0), cross(pa_there)
    wo_pass, pa_got = hold(wo_pass, pa_got)
    wo3 = cross(wo_pass)
    pre_own = lay((pa0, pa1, blk(pa_got, c, f_dev, 1), core(blk(pa_got, 1 - c, f_dev, 1))), 0, q)
    pre_up, pre_dn = along("y", 1)(pre_own), along("y", -1)(pre_own)
    slope = gelu_slope(f32(pre_own))
    g3, g1 = hold(g3, g1)
    op_a, op_b = hold(g3[:h], g1[h:])
    g2a, g2b = up(op_a), down(op_b)
    wo_mine, wo3 = hold(wo_mine, wo3)
    wo2 = cross(wo_mine)
    g2a, g2b, wo2, wo3, slope, pre_up, pre_dn = hold(g2a, g2b, wo2, wo3, slope, pre_up, pre_dn)
    og = lay_ring(g0, g3, g1, cat(g2a, g2b), z)
    hp = pre_own.shape[0] // 2
    og, pre_a, pre_b, l_in = hold(og, pre_up[:hp], pre_dn[hp:], layer_input)
    og_o, wo3 = core(og), core(wo3)
    pre_fa, pre_fb, ll = along("y", 1)(pre_a), along("y", -1)(pre_b), over("xl")(l_in)

    part = (dot_nt(og, cat(wo0, wo2, axis=1)) + dot_nt(og_o, cat(wo1, wo3, axis=1))).astype(BF)
    part, w_in, og, og_o, pre_fa, pre_fb, ll = hold(part, w_in, og, og_o, pre_fa, pre_fb, ll)
    act_grad = lax.psum_scatter(part, "y", scatter_dimension=0, tiled=True)
    wi_here, wi_there = blk(w_in, xh, 2 * f_dev, 1), blk(w_in, 1 - xh, 2 * f_dev, 1)
    first = xl == 0
    l_rows = cat(jnp.where(first, l_in, ll), jnp.where(first, ll, l_in))
    lh = cross(l_rows)
    wi_got = cross(wi_there)
    wi1 = core(blk(wi_here, 1 - c, f_dev, 1))
    pre = lay_ring(pre_own, pre_up, pre_dn, cat(pre_fa, pre_fb), y)
    act = gelu_act(f32(pre)).astype(BF)
    go = dot_tn(act, og).astype(BF)
    goo = dot_tn(act, og_o).astype(BF)
    wog_far = cat(go[:, d_own:], goo[:, d_own:], axis=1)
    act_grad, li0, wog_far, wi_got = hold(act_grad, cat(l_rows, lh, axis=1), wog_far, wi_got)
    h0 = (f32(act_grad) * slope).astype(BF)

    h0, li0, wog_far = hold(h0, li0, wog_far)
    wog_got = cross(wog_far)
    hidden = lax.all_gather(h0, "y", axis=0, tiled=True)
    li3, li1 = hold(up(li0), down(li0))
    op_a, op_b = hold(li3[:h], li1[h:])
    li2a, li2b, wog_got = hold(up(op_a), down(op_b), wog_got)
    wi3 = core(blk(wi_got, 1 - c, f_dev, 1))
    va, vb = cat(blk(wi_here, c, f_dev, 1), blk(wi_got, c, f_dev, 1)), cat(wi1, wi3)
    li = lay_ring(li0, li3, li1, cat(li2a, li2b), z)
    li_o = core(li)
    hidden, va, vb, goo, wog_got, li, li_o = hold(hidden, va, vb, goo, wog_got, li, li_o)

    n = hidden.shape[0] // 2
    ig_a, ig_b = core(dot_nt(hidden[:n], vb).astype(BF)), core(dot_nt(hidden[n:], vb).astype(BF))
    ig = (hold(dot_nt(hidden, va), hidden)[0] + f32(cat(ig_a, ig_b))).astype(BF)
    ig, hidden, goo, wog_got, li, og = hold(ig, hidden, goo, wog_got, li, og)
    ig = lax.psum_scatter(ig, "z", scatter_dimension=0, tiled=True)
    w3 = dot_tn(li_o[:, d_own:], hidden).astype(BF)
    w3, h_far = hold(w3, hidden)
    wig_far = cat(dot_tn(li[:, d_own:], h_far).astype(BF), core(w3))
    b0 = jnp.sum(f32(hidden), axis=0)
    b1 = core(b0)
    b23 = cross(jnp.stack([b0, b1]))
    wig_far, b23, go, goo, wog_got, og = hold(wig_far, b23, go, goo, wog_got, og)
    wig_got = cross(wig_far)
    h_near = hold(hidden, wig_far)[0]
    w0, w1 = dot_tn(li[:, :d_own], h_near).astype(BF), core(dot_tn(li_o[:, :d_own], h_near).astype(BF))
    wog_rec = core(cat(goo[:, :d_own], wog_got[:, d_own:], axis=1))
    w_out_grad = lay((go[:, :d_own], wog_rec[:, :d_own], wog_got[:, :d_own], wog_rec[:, d_own:]), 0, q)
    bias_in = lay((b0, b1, b23[0], b23[1]), 0, q)
    bias_out = jnp.sum(f32(og[:, :d_own]), axis=0)
    w_in_grad = jnp.zeros(w_in.shape, BF)
    for d, part in ((0, w0), (1, w1)):
        w_in_grad = put(w_in_grad, part, q ^ d, 1)
    ig, w_out_grad, bias_in, bias_out, w_in_grad = hold(ig, w_out_grad, bias_in, bias_out, w_in_grad)

    near, other = blk(ig, xl, t_own, 0), blk(ig, 1 - xl, t_own, 0)
    op_a, op_b, op_c, wig_got = hold(other[:, :d_own], near[:, d_own:], other[:, d_own:], wig_got)
    il, ih, ib = hold(over("xl")(op_a), cross(op_b), over("xl", "xh")(op_c))
    for d, part in ((2, wig_got[:d_own]), (3, wig_got[d_own:])):
        w_in_grad = put(w_in_grad, part, q ^ d, 1)
    input_grad = (f32(near[:, :d_own]) + f32(il) + f32(ih) + f32(ib)).astype(BF)
    return input_grad, w_in_grad, w_out_grad, bias_in, bias_out


def solution(mesh):
    fine = Mesh(mesh.devices.reshape(tuple(SIZES.values())), tuple(SIZES))
    row, col = ("z", "xl"), ("y", "xh", "c")
    in_specs = (P(row, col), P(row, col), P(col, row), P(col, row), P(row, col))
    out_specs = (P(row, col), P(col, row), P(row, col), P(row), P(col))
    return jax.shard_map(local, mesh=fine, in_specs=in_specs, out_specs=out_specs, check_vma=False)
```

```python
import jax
import jax.numpy as jnp
from jax import lax
from jax.sharding import Mesh, PartitionSpec as P

SIZES = {"z": 4, "xl": 2, "y": 4, "xh": 2, "c": 2}
BF, F32 = jnp.bfloat16, jnp.float32


def gelu_act(v):
    return v * (0.5 * (1.0 + lax.erf(v * 0.7071067811865476)))


def gelu_slope(v):
    normal_cdf = 0.5 * (1.0 + lax.erf(v * 0.7071067811865476))
    normal_pdf = jnp.exp(-0.5 * v * v) * 0.3989422804014327
    return normal_cdf + v * normal_pdf


def shift(x, axis, by):
    n = SIZES[axis]
    return lax.ppermute(x, axis, [(i, (i + by) % n) for i in range(n)])


def flip(x, *axes):
    n = 2 ** len(axes)
    return lax.ppermute(x, axes if len(axes) > 1 else axes[0], [(i, n - 1 - i) for i in range(n)])


def dot_nt(a, b):
    return lax.dot_general(a, b, (((1,), (1,)), ((), ())), preferred_element_type=F32)


def dot_tn(a, b):
    return lax.dot_general(a, b, (((0,), (0,)), ((), ())), preferred_element_type=F32)


def blk(x, i, size, axis):
    return lax.dynamic_slice_in_dim(x, i * size, size, axis)


def put(buf, x, i, axis):
    return lax.dynamic_update_slice_in_dim(buf, x, i * x.shape[axis], axis)


def hold(*xs):
    return lax.optimization_barrier(xs)


def phase(tokens, *items):
    held = hold(*(x for _, x in items), *tokens)
    return [send(x) for (send, _), x in zip(items, held)]


def along(axis, by):
    return lambda x: shift(x, axis, by)


def both_ways(axis, a, b):
    a, b = hold(a, b)
    return hold(shift(a, axis, 1), shift(b, axis, -1))


def over(*axes):
    return lambda x: flip(x, *axes)


def lay(parts, axis, q):
    shape = list(parts[0].shape)
    shape[axis] *= 4
    out = jnp.zeros(shape, parts[0].dtype)
    for d, part in enumerate(parts):
        out = put(out, part, q ^ d, axis)
    return out


def lay_ring(x, up, down, far, me):
    out = jnp.zeros((4 * x.shape[0], x.shape[1]), x.dtype)
    for k, part in ((0, x), (3, up), (1, down), (2, far)):
        out = put(out, part, (me + k) % 4, 0)
    return out


def ring_blocks(p, me):
    n = p.shape[0] // 4
    return [blk(p, (me + k) % 4, n, 0) for k in range(4)]


def x_join(g, gl, gh, gb, xl):
    first = xl == 0
    top = jnp.concatenate([jnp.where(first, g, gl), jnp.where(first, gh, gb)], 1)
    low = jnp.concatenate([jnp.where(first, gl, g), jnp.where(first, gb, gh)], 1)
    return jnp.concatenate([top, low], 0)


def pick(x, i):
    return lax.dynamic_index_in_dim(x, i, 0, keepdims=False)


def cat(*xs, axis=0):
    return jnp.concatenate(xs, axis)


def local(layer_input, out_grad, pre_act, w_in, w_out):
    z, xl, y, xh, c = (lax.axis_index(a) for a in ("z", "xl", "y", "xh", "c"))
    q = xh * 2 + c
    t_own, d_own = layer_input.shape
    f_dev = w_out.shape[0] // 4
    core, cross = over("c"), over("xh")
    f32 = lambda x: x.astype(F32)
    up, down = along("z", 1), along("z", -1)

    gl, gh, gb = over("xl")(out_grad), cross(out_grad), over("xl", "xh")(out_grad)
    wo4 = w_out.reshape(2, 2, f_dev, d_own)
    wo_here, wo_there = pick(wo4, xh), pick(wo4, 1 - xh)
    pa_here, pa_there = blk(pre_act, xh, 2 * f_dev, 1), blk(pre_act, 1 - xh, 2 * f_dev, 1)
    wo0, wo1 = pick(wo_here, c), core(pick(wo_here, 1 - c))
    wo_mine, wo_pass = pick(wo_there, c), pick(wo_there, 1 - c)
    pa0, pa1 = blk(pa_here, c, f_dev, 1), core(blk(pa_here, 1 - c, f_dev, 1))
    g0 = x_join(out_grad, gl, gh, gb, xl)
    h = g0.shape[0] // 2

    g0, pa_there, wo_mine, wo_pass, pa0, wo1 = hold(g0, pa_there, wo_mine, wo_pass, pa0, wo1)
    g3, g1, pa_got = up(g0), down(g0), cross(pa_there)
    wo_pass, pa_got = hold(wo_pass, pa_got)
    wo3 = cross(wo_pass)
    pre_own = lay((pa0, pa1, blk(pa_got, c, f_dev, 1), core(blk(pa_got, 1 - c, f_dev, 1))), 0, q)
    pre_up, pre_dn = along("y", 1)(pre_own), along("y", -1)(pre_own)
    slope = gelu_slope(f32(pre_own))
    g3, g1 = hold(g3, g1)
    op_a, op_b = hold(g3[:h], g1[h:])
    g2a, g2b = up(op_a), down(op_b)
    wo_mine, wo3 = hold(wo_mine, wo3)
    wo2 = cross(wo_mine)
    g2a, g2b, wo2, wo3, slope, pre_up, pre_dn = hold(g2a, g2b, wo2, wo3, slope, pre_up, pre_dn)
    og = lay_ring(g0, g3, g1, cat(g2a, g2b), z)
    hp = pre_own.shape[0] // 2
    og, pre_a, pre_b, l_in = hold(og, pre_up[:hp], pre_dn[hp:], layer_input)
    og_o, wo3 = core(og), core(wo3)
    pre_fa, pre_fb, ll = along("y", 1)(pre_a), along("y", -1)(pre_b), over("xl")(l_in)

    part = (dot_nt(og, cat(wo0, wo2, axis=1)) + dot_nt(og_o, cat(wo1, wo3, axis=1))).astype(BF)
    part, w_in, og, og_o, pre_fa, pre_fb, ll = hold(part, w_in, og, og_o, pre_fa, pre_fb, ll)
    act_grad = lax.psum_scatter(part, "y", scatter_dimension=0, tiled=True)
    wi_here, wi_there = blk(w_in, xh, 2 * f_dev, 1), blk(w_in, 1 - xh, 2 * f_dev, 1)
    first = xl == 0
    l_rows = cat(jnp.where(first, l_in, ll), jnp.where(first, ll, l_in))
    lh = cross(l_rows)
    wi_got = cross(wi_there)
    wi1 = core(blk(wi_here, 1 - c, f_dev, 1))
    pre = lay_ring(pre_own, pre_up, pre_dn, cat(pre_fa, pre_fb), y)
    act = gelu_act(f32(pre)).astype(BF)
    go3, act = hold(dot_tn(act, og_o[:, d_own:]).astype(BF), act)
    wog_far = cat(dot_tn(act, og[:, d_own:]).astype(BF), core(go3))
    go0, go1 = dot_tn(act, og[:, :d_own]).astype(BF), core(dot_tn(act, og_o[:, :d_own]).astype(BF))
    act_grad, li0, wog_far, wi_got = hold(act_grad, cat(l_rows, lh, axis=1), wog_far, wi_got)
    h0 = (f32(act_grad) * slope).astype(BF)

    h0, li0, wog_far = hold(h0, li0, wog_far)
    wog_got = cross(wog_far)
    hidden = lax.all_gather(h0, "y", axis=0, tiled=True)
    li3, li1 = hold(up(li0), down(li0))
    op_a, op_b = hold(li3[:h], li1[h:])
    li2a, li2b, wog_got = hold(up(op_a), down(op_b), wog_got)
    wi3 = core(blk(wi_got, 1 - c, f_dev, 1))
    va, vb = cat(blk(wi_here, c, f_dev, 1), blk(wi_got, c, f_dev, 1)), cat(wi1, wi3)
    li = lay_ring(li0, li3, li1, cat(li2a, li2b), z)
    li_o = core(li)
    hidden, va, vb, go0, go1, wog_got, li, li_o = hold(hidden, va, vb, go0, go1, wog_got, li, li_o)

    n = hidden.shape[0] // 2
    ig_a, ig_b = core(dot_nt(hidden[:n], vb).astype(BF)), core(dot_nt(hidden[n:], vb).astype(BF))
    ig = (hold(dot_nt(hidden, va), hidden)[0] + f32(cat(ig_a, ig_b))).astype(BF)
    ig, hidden, go0, go1, wog_got, li, og = hold(ig, hidden, go0, go1, wog_got, li, og)
    ig = lax.psum_scatter(ig, "z", scatter_dimension=0, tiled=True)
    w3 = dot_tn(li_o[:, d_own:], hidden).astype(BF)
    w3, h_far = hold(w3, hidden)
    wig_far = cat(dot_tn(li[:, d_own:], h_far).astype(BF), core(w3))
    b0 = jnp.sum(f32(hidden), axis=0)
    b1 = core(b0)
    b23 = cross(jnp.stack([b0, b1]))
    wig_far, b23, go0, go1, wog_got, og = hold(wig_far, b23, go0, go1, wog_got, og)
    wig_got = cross(wig_far)
    h_near = hold(hidden, wig_far)[0]
    w0, w1 = dot_tn(li[:, :d_own], h_near).astype(BF), core(dot_tn(li_o[:, :d_own], h_near).astype(BF))
    w_out_grad = lay((go0, go1, wog_got[:f_dev], wog_got[f_dev:]), 0, q)
    bias_in = lay((b0, b1, b23[0], b23[1]), 0, q)
    bias_out = jnp.sum(f32(og[:, :d_own]), axis=0)
    w_in_grad = jnp.zeros(w_in.shape, BF)
    for d, part in ((0, w0), (1, w1)):
        w_in_grad = put(w_in_grad, part, q ^ d, 1)
    ig, w_out_grad, bias_in, bias_out, w_in_grad = hold(ig, w_out_grad, bias_in, bias_out, w_in_grad)

    near, other = blk(ig, xl, t_own, 0), blk(ig, 1 - xl, t_own, 0)
    op_a, op_b, op_c, wig_got = hold(other[:, :d_own], near[:, d_own:], other[:, d_own:], wig_got)
    il, ih, ib = hold(over("xl")(op_a), cross(op_b), over("xl", "xh")(op_c))
    for d, part in ((2, wig_got[:d_own]), (3, wig_got[d_own:])):
        w_in_grad = put(w_in_grad, part, q ^ d, 1)
    input_grad = (f32(near[:, :d_own]) + f32(il) + f32(ih) + f32(ib)).astype(BF)
    return input_grad, w_in_grad, w_out_grad, bias_in, bias_out


def solution(mesh):
    fine = Mesh(mesh.devices.reshape(tuple(SIZES.values())), tuple(SIZES))
    row, col = ("z", "xl"), ("y", "xh", "c")
    in_specs = (P(row, col), P(row, col), P(col, row), P(col, row), P(row, col))
    out_specs = (P(row, col), P(col, row), P(row, col), P(row), P(col))
    return jax.shard_map(local, mesh=fine, in_specs=in_specs, out_specs=out_specs, check_vma=False)
```

```python
import jax
import jax.numpy as jnp
from jax import lax
from jax.sharding import Mesh, PartitionSpec as P

SIZES = {"z": 4, "xl": 2, "y": 4, "xh": 2, "c": 2}
BF, F32 = jnp.bfloat16, jnp.float32


def gelu_act(v):
    return v * (0.5 * (1.0 + lax.erf(v * 0.7071067811865476)))


def gelu_slope(v):
    normal_cdf = 0.5 * (1.0 + lax.erf(v * 0.7071067811865476))
    normal_pdf = jnp.exp(-0.5 * v * v) * 0.3989422804014327
    return normal_cdf + v * normal_pdf


def shift(x, axis, by):
    n = SIZES[axis]
    return lax.ppermute(x, axis, [(i, (i + by) % n) for i in range(n)])


def flip(x, *axes):
    n = 2 ** len(axes)
    return lax.ppermute(x, axes if len(axes) > 1 else axes[0], [(i, n - 1 - i) for i in range(n)])


def dot_nt(a, b):
    return lax.dot_general(a, b, (((1,), (1,)), ((), ())), preferred_element_type=F32)


def dot_tn(a, b):
    return lax.dot_general(a, b, (((0,), (0,)), ((), ())), preferred_element_type=F32)


def blk(x, i, size, axis):
    return lax.dynamic_slice_in_dim(x, i * size, size, axis)


def put(buf, x, i, axis):
    return lax.dynamic_update_slice_in_dim(buf, x, i * x.shape[axis], axis)


def hold(*xs):
    return lax.optimization_barrier(xs)


def phase(tokens, *items):
    held = hold(*(x for _, x in items), *tokens)
    return [send(x) for (send, _), x in zip(items, held)]


def along(axis, by):
    return lambda x: shift(x, axis, by)


def both_ways(axis, a, b):
    a, b = hold(a, b)
    return hold(shift(a, axis, 1), shift(b, axis, -1))


def over(*axes):
    return lambda x: flip(x, *axes)


def lay(parts, axis, q):
    shape = list(parts[0].shape)
    shape[axis] *= 4
    out = jnp.zeros(shape, parts[0].dtype)
    for d, part in enumerate(parts):
        out = put(out, part, q ^ d, axis)
    return out


def lay_ring(x, up, down, far, me):
    out = jnp.zeros((4 * x.shape[0], x.shape[1]), x.dtype)
    for k, part in ((0, x), (3, up), (1, down), (2, far)):
        out = put(out, part, (me + k) % 4, 0)
    return out


def ring_blocks(p, me):
    n = p.shape[0] // 4
    return [blk(p, (me + k) % 4, n, 0) for k in range(4)]


def x_join(g, gl, gh, gb, xl):
    first = xl == 0
    top = jnp.concatenate([jnp.where(first, g, gl), jnp.where(first, gh, gb)], 1)
    low = jnp.concatenate([jnp.where(first, gl, g), jnp.where(first, gb, gh)], 1)
    return jnp.concatenate([top, low], 0)


def pick(x, i):
    return lax.dynamic_index_in_dim(x, i, 0, keepdims=False)


def cat(*xs, axis=0):
    return jnp.concatenate(xs, axis)


def local(layer_input, out_grad, pre_act, w_in, w_out):
    z, xl, y, xh, c = (lax.axis_index(a) for a in ("z", "xl", "y", "xh", "c"))
    q = xh * 2 + c
    t_own, d_own = layer_input.shape
    f_dev = w_out.shape[0] // 4
    core, cross = over("c"), over("xh")
    f32 = lambda x: x.astype(F32)
    up, down = along("z", 1), along("z", -1)

    gl, gh, gb = over("xl")(out_grad), cross(out_grad), over("xl", "xh")(out_grad)
    wo4 = w_out.reshape(2, 2, f_dev, d_own)
    wo_here, wo_there = pick(wo4, xh), pick(wo4, 1 - xh)
    pa_here, pa_there = blk(pre_act, xh, 2 * f_dev, 1), blk(pre_act, 1 - xh, 2 * f_dev, 1)
    wo0, wo1 = pick(wo_here, c), core(pick(wo_here, 1 - c))
    wo_mine, wo_pass = pick(wo_there, c), pick(wo_there, 1 - c)
    pa0, pa1 = blk(pa_here, c, f_dev, 1), core(blk(pa_here, 1 - c, f_dev, 1))
    g0 = x_join(out_grad, gl, gh, gb, xl)
    h = g0.shape[0] // 2

    g0, pa_there, wo_mine, wo_pass, pa0, wo1 = hold(g0, pa_there, wo_mine, wo_pass, pa0, wo1)
    g3, g1, pa_got = up(g0), down(g0), cross(pa_there)
    wo_pass, pa_got = hold(wo_pass, pa_got)
    wo3 = cross(wo_pass)
    pre_own = lay((pa0, pa1, blk(pa_got, c, f_dev, 1), core(blk(pa_got, 1 - c, f_dev, 1))), 0, q)
    pre_up, pre_dn = along("y", 1)(pre_own), along("y", -1)(pre_own)
    slope = gelu_slope(f32(pre_own))
    g3, g1 = hold(g3, g1)
    op_a, op_b = hold(g3[:h], g1[h:])
    g2a, g2b = up(op_a), down(op_b)
    wo_mine, wo3 = hold(wo_mine, wo3)
    wo2 = cross(wo_mine)
    g2a, g2b, wo2, wo3, slope, pre_up, pre_dn = hold(g2a, g2b, wo2, wo3, slope, pre_up, pre_dn)
    og = lay_ring(g0, g3, g1, cat(g2a, g2b), z)
    hp = pre_own.shape[0] // 2
    og, pre_a, pre_b, l_in = hold(og, pre_up[:hp], pre_dn[hp:], layer_input)
    og_o, wo3 = core(og), core(wo3)
    pre_fa, pre_fb, ll = along("y", 1)(pre_a), along("y", -1)(pre_b), over("xl")(l_in)

    part = (dot_nt(og, cat(wo0, wo2, axis=1)) + dot_nt(og_o, cat(wo1, wo3, axis=1))).astype(BF)
    part, w_in, og, og_o, pre_fa, pre_fb, ll = hold(part, w_in, og, og_o, pre_fa, pre_fb, ll)
    act_grad = lax.psum_scatter(part, "y", scatter_dimension=0, tiled=True)
    wi_here, wi_there = blk(w_in, xh, 2 * f_dev, 1), blk(w_in, 1 - xh, 2 * f_dev, 1)
    first = xl == 0
    l_rows = cat(jnp.where(first, l_in, ll), jnp.where(first, ll, l_in))
    pre = lay_ring(pre_own, pre_up, pre_dn, cat(pre_fa, pre_fb), y)
    l_rows, wi_there, pre = hold(l_rows, wi_there, pre)
    lh = cross(l_rows)
    wi_got = cross(wi_there)
    wi1 = core(blk(wi_here, 1 - c, f_dev, 1))
    act = gelu_act(f32(pre)).astype(BF)
    go3, act = hold(dot_tn(act, og_o[:, d_own:]).astype(BF), act)
    wog_far = cat(dot_tn(act, og[:, d_own:]).astype(BF), core(go3))
    go0, go1 = dot_tn(act, og[:, :d_own]).astype(BF), core(dot_tn(act, og_o[:, :d_own]).astype(BF))
    act_grad, li0, wog_far, wi_got = hold(act_grad, cat(l_rows, lh, axis=1), wog_far, wi_got)
    h0 = (f32(act_grad) * slope).astype(BF)

    h0, li0, wog_far = hold(h0, li0, wog_far)
    wog_got = cross(wog_far)
    hidden = lax.all_gather(h0, "y", axis=0, tiled=True)
    li3, li1 = hold(up(li0), down(li0))
    op_a, op_b = hold(li3[:h], li1[h:])
    li2a, li2b, wog_got = hold(up(op_a), down(op_b), wog_got)
    wi3 = core(blk(wi_got, 1 - c, f_dev, 1))
    va, vb = cat(blk(wi_here, c, f_dev, 1), blk(wi_got, c, f_dev, 1)), cat(wi1, wi3)
    li = lay_ring(li0, li3, li1, cat(li2a, li2b), z)
    li_o = core(li)
    hidden, va, vb, go0, go1, wog_got, li, li_o = hold(hidden, va, vb, go0, go1, wog_got, li, li_o)

    n = hidden.shape[0] // 2
    ig_a, ig_b = core(dot_nt(hidden[:n], vb).astype(BF)), core(dot_nt(hidden[n:], vb).astype(BF))
    ig = (hold(dot_nt(hidden, va), hidden)[0] + f32(cat(ig_a, ig_b))).astype(BF)
    ig, hidden, go0, go1, wog_got, li, og = hold(ig, hidden, go0, go1, wog_got, li, og)
    ig = lax.psum_scatter(ig, "z", scatter_dimension=0, tiled=True)
    w3 = dot_tn(li_o[:, d_own:], hidden).astype(BF)
    w3, h_far = hold(w3, hidden)
    wig_far = cat(dot_tn(li[:, d_own:], h_far).astype(BF), core(w3))
    b0 = jnp.sum(f32(hidden), axis=0)
    b1 = core(b0)
    b23 = cross(jnp.stack([b0, b1]))
    wig_far, b23, go0, go1, wog_got, og = hold(wig_far, b23, go0, go1, wog_got, og)
    wig_got = cross(wig_far)
    h_near = hold(hidden, wig_far)[0]
    w0, w1 = dot_tn(li[:, :d_own], h_near).astype(BF), core(dot_tn(li_o[:, :d_own], h_near).astype(BF))
    w_out_grad = lay((go0, go1, wog_got[:f_dev], wog_got[f_dev:]), 0, q)
    bias_in = lay((b0, b1, b23[0], b23[1]), 0, q)
    bias_out = jnp.sum(f32(og[:, :d_own]), axis=0)
    w_in_grad = jnp.zeros(w_in.shape, BF)
    for d, part in ((0, w0), (1, w1)):
        w_in_grad = put(w_in_grad, part, q ^ d, 1)
    ig, w_out_grad, bias_in, bias_out, w_in_grad = hold(ig, w_out_grad, bias_in, bias_out, w_in_grad)

    near, other = blk(ig, xl, t_own, 0), blk(ig, 1 - xl, t_own, 0)
    op_a, op_b, op_c, wig_got = hold(other[:, :d_own], near[:, d_own:], other[:, d_own:], wig_got)
    il, ih, ib = hold(over("xl")(op_a), cross(op_b), over("xl", "xh")(op_c))
    for d, part in ((2, wig_got[:d_own]), (3, wig_got[d_own:])):
        w_in_grad = put(w_in_grad, part, q ^ d, 1)
    input_grad = (f32(near[:, :d_own]) + f32(il) + f32(ih) + f32(ib)).astype(BF)
    return input_grad, w_in_grad, w_out_grad, bias_in, bias_out


def solution(mesh):
    fine = Mesh(mesh.devices.reshape(tuple(SIZES.values())), tuple(SIZES))
    row, col = ("z", "xl"), ("y", "xh", "c")
    in_specs = (P(row, col), P(row, col), P(col, row), P(col, row), P(row, col))
    out_specs = (P(row, col), P(col, row), P(row, col), P(row), P(col))
    return jax.shard_map(local, mesh=fine, in_specs=in_specs, out_specs=out_specs, check_vma=False)
```
